32 devices in a mesh: dom: 4 (over y, core), space: 8 (over z, x).
Axes of the slice: x: 2, y: 2, z: 4, core: 2. Of those that a mesh axis runs over, the one named last changes fastest.
Arguments:
- orbitals: bfloat16 [4, 2, 32, 16, 8, 128], P('dom', None, 'space'), may hold values from -6 to 6
- initial: bfloat16 [4, 2, 32, 16, 8, 128], P('dom', None, 'space'), may hold values from -4 to 4
- potential: float32 [4, 32, 128], P('dom', 'space'), may hold values from -1 to 1
- external: float32 [4, 32, 128], P('dom', 'space'), may hold values from -1 to 1
- occupation: float32 [128], replicated, may hold values from 0.5 to 2
- coupling: float32 [128, 128], replicated, may hold values from -1.25 to 1.25
- neighbours: int32 [4, 2], replicated, may hold values from 0 to 3, as said below
- offsets: int32 [4, 2], replicated, may hold values from 0 to 12
Outputs:
- evolved: bfloat16 [4, 2, 32, 16, 8, 128], P('dom', None, 'space')
- intersection: float32 [4, 2, 128, 128], P('dom')
- new_potential: float32 [4, 32, 128], P('dom', 'space')
The draws below stay inside these ranges and needn't reach their ends.
Inputs may be any that keep to these rules, and one draw needn't show every extreme that they name: Following upper neighbours visits all 4 domains in one cycle, and the lower neighbour of a domain's upper neighbour is that domain.
All inputs are finite; a program needn't handle non-finite values.
Results may differ from the reference program's by a relative error of at most 0.007.
Values may be sent and summed in bfloat16 or wider, within the bound.
A program may use at most 64 MiB of HBM per device.

```python
import jax
import jax.numpy as jnp
from jax import lax

NORB = 128
GY = 16
GZ = 8
TAYLOR = 4
STEPS = 2
BUF = 4
NDOM = 4
GX = 32
NCELLS = 4096


def orbital_pair(key):
    shape = (NDOM, 2, GX, GY, GZ, NORB)
    key_base = jax.random.fold_in(key, 101)
    key_noise = jax.random.fold_in(key, 102)
    key_real = jax.random.fold_in(key, 103)
    key_imag = jax.random.fold_in(key, 104)
    key_center = jax.random.fold_in(key, 106)
    base = jax.random.truncated_normal(key_base, -4.0, 4.0, shape, jnp.float32) * 0.7071
    noise = jax.random.truncated_normal(key_noise, -4.0, 4.0, shape, jnp.float32)
    centers = jax.random.uniform(key_center, (NDOM, NORB), jnp.float32, 0.0, 1.0 * GX)
    planes = jnp.arange(GX, dtype=jnp.float32)
    distance = (planes[None, :, None] - centers[:, None, :]) / (0.1 * GX)
    envelope = 0.25 + 1.75 * jnp.exp(-0.5 * distance * distance)
    envelope = envelope.reshape(NDOM, 1, GX, 1, 1, NORB)
    base = jnp.clip(base * envelope, -4.0, 4.0)
    spread = 0.5 / NORB ** 0.5
    mix_real = 0.7 * jnp.eye(NORB, dtype=jnp.float32) + spread * jax.random.normal(key_real, (NDOM, NORB, NORB), jnp.float32)
    mix_imag = spread * jax.random.normal(key_imag, (NDOM, NORB, NORB), jnp.float32)
    form = 'dxyzn,dnm->dxyzm'
    high = lax.Precision.HIGHEST
    part_real = jnp.einsum(form, base[:, 0], mix_real, precision=high) - jnp.einsum(form, base[:, 1], mix_imag, precision=high)
    part_imag = jnp.einsum(form, base[:, 0], mix_imag, precision=high) + jnp.einsum(form, base[:, 1], mix_real, precision=high)
    current = jnp.clip(jnp.stack([part_real, part_imag], axis=1) + 0.5 * noise, -6.0, 6.0)
    return (base, current)


def draw_orbitals(key, part):
    base, current = orbital_pair(key)
    return current.astype(jnp.bfloat16)


def draw_initial(key, part):
    base, current = orbital_pair(key)
    return base.astype(jnp.bfloat16)


def draw_neighbours(key, part):
    order = jax.random.permutation(jax.random.fold_in(key, 7), NDOM).astype(jnp.int32)
    upper = jnp.roll(order, -1)
    lower = jnp.roll(order, 1)
    table = jnp.zeros((NDOM, 2), jnp.int32)
    table = table.at[order, 0].set(lower)
    table = table.at[order, 1].set(upper)
    return table


def plant(array, key, low, top_value):
    place = [jax.random.randint(jax.random.fold_in(key, axis), (), 0, length) for axis, length in enumerate(array.shape)]
    main_axis = array.shape.index(max(array.shape))
    beside = place[:main_axis] + [(place[main_axis] + 1) % array.shape[main_axis]] + place[main_axis + 1:]
    return array.at[tuple(place)].set(low).at[tuple(beside)].set(top_value)


def level_of(key, shape, pieces, low, high):
    def one(dim, shards_of):
        draws = jax.random.uniform(jax.random.fold_in(jax.random.fold_in(key, 6), dim), (shards_of,), jnp.float32, low / len(pieces), high / len(pieces))
        return jnp.repeat(jnp.exp(draws), shape[dim] // shards_of).reshape((-1,) + (1,) * (len(shape) - dim - 1))

    loudness = one(*pieces[0])
    for cut in pieces[1:]:
        loudness = loudness * one(*cut)
    return loudness


def scatter_about(rng, dims, scale, most, held_as=jnp.bfloat16):
    result = scale * jax.random.normal(rng, dims, jnp.float32)
    return jnp.clip(result, min=-most, max=most).astype(held_as)


def setup_inputs(seed: int = 0) -> dict:
    key_list = jax.random.split(jax.random.key(seed), 9)
    return {
        "orbitals": draw_orbitals(jax.random.fold_in(key_list[8], 71), 0),
        "initial": draw_initial(jax.random.fold_in(key_list[8], 71), 0),
        "potential": jnp.clip(jax.random.uniform(key_list[2], (NDOM, GX, GY * GZ), jnp.float32, -1.0, 1.0) * level_of(key_list[2], (NDOM, GX, GY * GZ), ((0, 4), (1, 8)), -0.4, 0.0), -1.0, 1.0),
        "external": jnp.clip(jax.random.uniform(key_list[3], (NDOM, GX, GY * GZ), jnp.float32, -1.0, 1.0) * level_of(key_list[3], (NDOM, GX, GY * GZ), ((0, 4), (1, 8)), -0.4, 0.0), -1.0, 1.0),
        "occupation": jnp.clip(jax.random.uniform(key_list[4], (NORB,), jnp.float32, 0.5, 2.0), 0.5, 2.0),
        "coupling": scatter_about(key_list[5], (NORB, NORB), (10.0 / NORB), 1.25, jnp.float32),
        "neighbours": draw_neighbours(jax.random.fold_in(key_list[8], 71), 0),
        "offsets": plant(jax.random.randint(key_list[7], (NDOM, 2), 0, GY - BUF + 1), jax.random.fold_in(key_list[7], 1), 0, GY - BUF).astype(jnp.int32),
    }


time_step = 0.4
half_step = 0.2
xc_factor = 0.9847450218426965


def laplace(source):
    center = source[:, 1:-1]
    total = source[:, 2:] + source[:, :-2] - 6.0 * center
    padded = jnp.pad(center, ((0, 0), (0, 0), (1, 1), (1, 1), (0, 0)))
    total = total + padded[:, :, 2:, 1:-1] + padded[:, :, :-2, 1:-1]
    total = total + padded[:, :, 1:-1, 2:] + padded[:, :, 1:-1, :-2]
    return total


def phase_turn(field, angle):
    cosv = jnp.cos(angle)[..., None]
    sinv = jnp.sin(angle)[..., None]
    return jnp.stack([cosv * field[0] + sinv * field[1], cosv * field[1] - sinv * field[0]])


def kinetic(field):
    running = field
    taylor_term = lax.optimization_barrier(field.astype(jnp.bfloat16))
    for order in range(1, TAYLOR + 1):
        widened = jnp.pad(taylor_term.astype(jnp.float32), ((0, 0), (1, 1), (0, 0), (0, 0), (0, 0)))
        curvature = laplace(widened)
        factor = time_step / (2.0 * order)
        update = jnp.stack([-factor * curvature[1], factor * curvature[0]])
        running = running + update
        taylor_term = lax.optimization_barrier(update.astype(jnp.bfloat16))
    return running


def reference(orbitals, initial, potential, external, occupation, coupling, neighbours, offsets):
    def evolve(items):
        field_in, start, grid_pot = items
        field = field_in.astype(jnp.float32)
        angle = half_step * grid_pot.reshape(GX, GY, GZ)
        flat_start = start.reshape(-1, NORB)
        start_real = start[0].reshape(-1, NORB)
        start_imag = start[1].reshape(-1, NORB)
        intersection = jnp.zeros((2, NORB, NORB), jnp.float32)
        for section in range(STEPS):
            field = phase_turn(field, angle)
            field = kinetic(field)
            field = phase_turn(field, angle)
            rounded = field.astype(jnp.bfloat16)
            over_real = jnp.dot(flat_start.T, rounded.reshape(-1, NORB), preferred_element_type=jnp.float32)
            over_imag = jnp.dot(start_real.T, rounded[1].reshape(-1, NORB), preferred_element_type=jnp.float32) - jnp.dot(start_imag.T, rounded[0].reshape(-1, NORB), preferred_element_type=jnp.float32)
            intersection = jnp.stack([over_real, over_imag]) * (1.0 / NCELLS)
            mix_real = jnp.dot(coupling, intersection[0], precision=lax.Precision.HIGHEST).astype(jnp.bfloat16)
            mix_imag = jnp.dot(coupling, intersection[1], precision=lax.Precision.HIGHEST).astype(jnp.bfloat16)
            corr_real = jnp.dot(start_real, mix_real, preferred_element_type=jnp.float32) - jnp.dot(start_imag, mix_imag, preferred_element_type=jnp.float32)
            corr_imag = jnp.dot(start_real, mix_imag, preferred_element_type=jnp.float32) + jnp.dot(start_imag, mix_real, preferred_element_type=jnp.float32)
            shape_one = (GX, GY, GZ, NORB)
            field = field + time_step * jnp.stack([corr_imag.reshape(shape_one), -corr_real.reshape(shape_one)])
        density = jnp.sum(field * field * occupation, axis=(0, 4))
        return field, intersection, density

    fields, intersections, densities = lax.map(evolve, (orbitals, initial, potential))
    cut = lambda arr, start: lax.dynamic_slice_in_dim(arr, start, BUF, 1)
    lower_bricks = jax.vmap(cut)(densities[neighbours[:, 0]], offsets[:, 0].astype(jnp.int32))
    upper_bricks = jax.vmap(cut)(densities[neighbours[:, 1]], offsets[:, 1].astype(jnp.int32))
    planes = jnp.arange(BUF).astype(jnp.float32)
    weight_low = ((planes + 1.0) / (BUF + 1.0)).reshape(1, 1, BUF, 1)
    weight_high = ((BUF - planes) / (BUF + 1.0)).reshape(1, 1, BUF, 1)
    low = densities[:, :, :BUF] * weight_low + lower_bricks * (1.0 - weight_low)
    high = densities[:, :, GY - BUF:] * weight_high + upper_bricks * (1.0 - weight_high)
    blended = jnp.concatenate([low, densities[:, :, BUF:GY - BUF], high], axis=2)
    new_grid = external.reshape(NDOM, GX, GY, GZ) - xc_factor * jnp.cbrt(blended + 1e-6)

    def finish(items):
        field, grid_pot = items
        return phase_turn(field, half_step * grid_pot).astype(jnp.bfloat16)

    evolved = lax.map(finish, (fields, new_grid))
    return evolved, intersections, new_grid.reshape(NDOM, GX, GY * GZ)
```

```python
import functools

import jax
import jax.numpy as jnp
from jax import lax
from jax.experimental import pallas as pl
from jax.experimental.pallas import tpu as pltpu
from jax.sharding import PartitionSpec as P

TAYLOR = 4
STEPS = 2
BUF = 4

time_step = 0.4
half_step = 0.2
xc_factor = 0.9847450218426965

F32 = jnp.float32
BF16 = jnp.bfloat16
HALO = TAYLOR


def body(
    sizes,
    orb,
    ini,
    pot,
    ext,
    occ,
    coup,
    neigh,
    offs,
    evolved_out,
    inter_out,
    pot_out,
    packed,
    other_raw,
    halo_raw,
    other_ini,
    grids,
    source,
    term_a,
    term_b,
    cos_x,
    sin_x,
    field,
    odd,
    rounded,
    turned,
    sums,
    inter,
    dens,
    evolved,
    send_sem,
    recv_sem,
    sum_send,
    sum_recv,
    dens_send,
    dens_recv,
):
    doms, space, slab, rows_y, cols_z, norb = sizes
    cells = rows_y * cols_z
    pairs = space // 2
    half = norb // 2
    main = 2 * slab
    total = main + 2 * HALO
    rows = slab * cells
    edge = HALO * cells
    cells_total = space * rows

    dom = lax.axis_index("dom")
    place = lax.axis_index("space")
    pair = place // 2
    member = place % 2
    partner = (dom, 2 * pair + 1 - member)
    has_lower = pair > 0
    has_upper = pair < pairs - 1
    outward = pair + 2 * member - 1
    has_outward = jnp.logical_and(outward >= 0, outward < pairs)

    def copy(src, dst, ss, rs, device):
        return pltpu.make_async_remote_copy(
            src_ref=src,
            dst_ref=dst,
            send_sem=ss,
            recv_sem=rs,
            device_id=device,
            device_id_type=pl.DeviceIdType.MESH,
        )

    def arrived(dst, rs):
        copy(dst, dst, send_sem.at[0], rs, partner).wait_recv()

    barrier = pltpu.get_barrier_semaphore()

    def greet(device):
        pl.semaphore_signal(barrier, inc=1, device_id=device, device_id_type=pl.DeviceIdType.MESH)

    greet(partner)
    for step in range(1, pairs):
        greet((dom, 2 * ((pair + step) % pairs) + member))
    for step in range(1, doms):
        greet(((dom + step) % doms, 2 * pair))
        greet(((dom + step) % doms, 2 * pair + 1))

    @pl.when(has_outward)
    def _():
        greet((dom, 2 * outward + 1 - member))

    lane = lax.broadcasted_iota(jnp.int32, (cells, norb), 1)
    left = lane < half
    sign = jnp.where(left, -1.0, 1.0).astype(F32)

    def swap(value):
        return pltpu.roll(value, half, 1)

    def at(index, count=1):
        return pl.ds(pl.multiple_of(index * cells, cells), count * cells)

    def pack_plane(j, carry):
        re = orb[0, at(j), :].astype(F32)
        im = orb[1, at(j), :].astype(F32)
        packed[0, at(j), :] = jnp.where(left, re, swap(im)).astype(BF16)
        packed[1, at(j), :] = jnp.where(left, swap(re), im).astype(BF16)
        return carry

    lax.fori_loop(0, slab, pack_plane, 0)
    grids[0, 0:slab, :] = pot[...]
    grids[0, slab:, :] = ext[...]

    pl.semaphore_wait(barrier, pairs + 2 * (doms - 1) + has_outward.astype(jnp.int32))

    grid_swap = copy(grids.at[0], grids.at[1], send_sem.at[0], recv_sem.at[0], partner)
    grid_swap.start()
    role = 1 - member
    grid_edge = [
        copy(
            grids.at[0],
            grids.at[2 + role],
            send_sem.at[1 + k],
            recv_sem.at[1 + role],
            (dom, 2 * outward + k),
        )
        for k in range(2)
    ]
    first = pl.ds(pl.multiple_of(member * (rows - edge), cells), edge)
    raw_edge = [
        copy(
            packed.at[k, first],
            halo_raw.at[role],
            send_sem.at[3 + k],
            recv_sem.at[3 + role],
            (dom, 2 * outward + k),
        )
        for k in range(2)
    ]
    raw_swap = copy(packed.at[1 - member], other_raw, send_sem.at[5], recv_sem.at[5], partner)
    ini_swap = copy(ini, other_ini, send_sem.at[6], recv_sem.at[6], partner)

    @pl.when(has_outward)
    def _():
        for item in grid_edge + raw_edge:
            item.start()

    raw_swap.start()
    ini_swap.start()

    zero_edge = jnp.zeros((edge, norb), BF16)

    @pl.when(jnp.logical_not(has_lower))
    def _():
        grids[2] = jnp.zeros((2 * slab, cells), F32)
        halo_raw[0] = zero_edge
        source[1, 0:edge, :] = zero_edge

    @pl.when(jnp.logical_not(has_upper))
    def _():
        grids[3] = jnp.zeros((2 * slab, cells), F32)
        halo_raw[1] = zero_edge
        source[1, edge + main * cells :, :] = zero_edge

    def spread(angle, first_plane):
        count = angle.shape[0]
        fill = jnp.zeros((norb - 2 * count, cells), F32)
        table = jnp.concatenate([jnp.cos(angle), jnp.sin(angle), fill], axis=0).T
        for j in range(count):
            here = slice((first_plane + j) * cells, (first_plane + j + 1) * cells)
            cos_x[here, :] = jnp.broadcast_to(table[:, j : j + 1], (cells, norb))
            column = table[:, count + j : count + j + 1]
            sin_x[here, :] = jnp.broadcast_to(column, (cells, norb)) * sign

    arrived(grids.at[1], recv_sem.at[0])

    @pl.when(has_lower)
    def _():
        arrived(grids.at[2], recv_sem.at[1])

    @pl.when(has_upper)
    def _():
        arrived(grids.at[3], recv_sem.at[2])

    is_even = member == 0
    mine, theirs = grids[0], grids[1]
    low_grid = jnp.where(is_even, mine, theirs)
    high_grid = jnp.where(is_even, theirs, mine)
    spread(
        half_step
        * jnp.concatenate(
            [grids[2, slab - HALO : slab], low_grid[:slab], high_grid[:slab], grids[3, 0:HALO]],
            axis=0,
        ),
        0,
    )

    def phase(value, j):
        return cos_x[at(j), :] * value - sin_x[at(j), :] * swap(value)

    def begin_own(j, carry):
        plane = HALO + member * slab + j
        value = phase(packed[member, at(j), :].astype(F32), plane)
        field[at(plane - HALO), :] = value
        source[0, at(plane), :] = value.astype(BF16)
        return carry

    def begin_other(j, carry):
        plane = HALO + (1 - member) * slab + j
        value = phase(other_raw[at(j), :].astype(F32), plane)
        field[at(plane - HALO), :] = value
        source[0, at(plane), :] = value.astype(BF16)
        return carry

    def begin_lower(j, carry):
        source[0, at(j), :] = phase(halo_raw[0, at(j), :].astype(F32), j).astype(BF16)
        return carry

    def begin_upper(j, carry):
        plane = HALO + main + j
        source[0, at(plane), :] = phase(halo_raw[1, at(j), :].astype(F32), plane).astype(BF16)
        return carry

    lax.fori_loop(0, slab, begin_own, 0)

    @pl.when(has_lower)
    def _():
        arrived(halo_raw.at[0], recv_sem.at[3])

    @pl.when(has_upper)
    def _():
        arrived(halo_raw.at[1], recv_sem.at[4])

    lax.fori_loop(0, HALO, begin_lower, 0)
    lax.fori_loop(0, HALO, begin_upper, 0)
    arrived(other_raw, recv_sem.at[5])
    lax.fori_loop(0, slab, begin_other, 0)

    z_index = lax.broadcasted_iota(jnp.int32, (rows_y, cols_z, norb), 1)
    z_first = z_index == 0
    z_last = z_index == cols_z - 1
    zero_row = jnp.zeros((1, cols_z, norb), F32)
    lower_keep = has_lower.astype(F32)
    upper_keep = has_upper.astype(F32)

    def curvature(load, j):
        center = load(j).astype(F32).reshape(rows_y, cols_z, norb)
        outer = (load(j - 1).astype(F32) + load(j + 1).astype(F32)).reshape(center.shape)
        value = outer - 6.0 * center
        value = value + jnp.concatenate([center[1:], zero_row], axis=0)
        value = value + jnp.concatenate([zero_row, center[:-1]], axis=0)
        value = value + jnp.where(z_first, 0.0, pltpu.roll(center, 1, 1))
        value = value + jnp.where(z_last, 0.0, pltpu.roll(center, cols_z - 1, 1))
        return value.reshape(cells, norb)

    def kinetic(section):
        def load_source(j):
            return source[section, at(j), :]

        def load_a(j):
            return term_a[at(j), :]

        def load_b(j):
            return term_b[at(j), :]

        loads = [load_source, load_a, load_b, load_a]
        stores = [term_a, term_b, term_a]
        for order in range(1, TAYLOR + 1):
            load = loads[order - 1]
            factor = time_step / (2.0 * order)

            def edge_plane(j, keep, load=load, factor=factor, order=order):
                stores[order - 1][at(j), :] = ((factor * keep) * curvature(load, j)).astype(BF16)

            def lower(j, carry, edge_plane=edge_plane):
                edge_plane(j, lower_keep)
                return carry

            def upper(j, carry, edge_plane=edge_plane):
                edge_plane(j, upper_keep)
                return carry

            def middle(j, carry, load=load, factor=factor, order=order):
                update = factor * curvature(load, j)
                here = at(j - HALO)
                if order < TAYLOR:
                    stores[order - 1][at(j), :] = update.astype(BF16)
                if order == 1:
                    odd[here, :] = update
                elif order == 2:
                    field[here, :] = field[here, :] - update
                elif order == 3:
                    odd[here, :] = odd[here, :] - update
                else:
                    value = field[here, :] + update + sign * swap(odd[here, :])
                    value = phase(value, j)
                    field[here, :] = value
                    near = value.astype(BF16)
                    rounded[here, :] = near
                    turned[here, :] = (-sign * swap(near.astype(F32))).astype(BF16)
                return carry

            if order < TAYLOR:
                lax.fori_loop(order, HALO, lower, 0)
                lax.fori_loop(HALO + main, total - order, upper, 0)
            lax.fori_loop(HALO, HALO + main, middle, 0)

    own_rows = pl.ds(pl.multiple_of(member * rows, cells), rows)
    other_rows = pl.ds(pl.multiple_of((1 - member) * rows, cells), rows)

    def contract(a, b):
        return lax.dot_general(a, b, (((0,), (0,)), ((), ())), preferred_element_type=F32)

    def dot(a, b):
        return jnp.dot(a, b, preferred_element_type=F32)

    edge_sends = []
    sum_sends = []
    result = None
    for section in range(STEPS):
        if section > 0:

            def restart(j, carry):
                value = phase(field[at(j), :], HALO + j)
                field[at(j), :] = value
                source[1, at(HALO + j), :] = value.astype(BF16)
                return carry

            lax.fori_loop(0, main, restart, 0)
            down = copy(
                source.at[1, pl.ds(edge, edge)],
                source.at[1, pl.ds(edge + main * cells, edge)],
                send_sem.at[7],
                recv_sem.at[8],
                (dom, 2 * (pair - 1) + member),
            )
            up = copy(
                source.at[1, pl.ds(main * cells, edge)],
                source.at[1, pl.ds(0, edge)],
                send_sem.at[8],
                recv_sem.at[7],
                (dom, 2 * (pair + 1) + member),
            )

            @pl.when(has_lower)
            def _():
                down.start()

            @pl.when(has_upper)
            def _():
                up.start()

            @pl.when(has_lower)
            def _():
                arrived(source.at[1, pl.ds(0, edge)], recv_sem.at[7])

            @pl.when(has_upper)
            def _():
                arrived(source.at[1, pl.ds(edge + main * cells, edge)], recv_sem.at[8])

            edge_sends = [down, up]
        kinetic(section)
        part = contract(ini[0], rounded[own_rows, :]) + contract(ini[1], turned[own_rows, :])
        if section == 0:
            arrived(other_ini, recv_sem.at[6])
        part = part + contract(other_ini[0], rounded[other_rows, :])
        part = part + contract(other_ini[1], turned[other_rows, :])
        sums[section, pair] = (part * (1.0 / cells_total)).astype(sums.dtype)
        for step in range(1, pairs):
            item = copy(
                sums.at[section, pair],
                sums.at[section, pair],
                sum_send.at[section, step],
                sum_recv.at[section, pair],
                (dom, 2 * ((pair + step) % pairs) + member),
            )
            item.start()
            sum_sends.append(item)
        for step in range(1, pairs):
            slot = (pair + step) % pairs
            arrived(sums.at[section, slot], sum_recv.at[section, slot])
        result = sums[section, 0].astype(F32)
        for slot in range(1, pairs):
            result = result + sums[section, slot].astype(F32)
        if section == STEPS - 1:
            inter[member] = result
            inter_swap = copy(
                inter.at[member], inter.at[member], send_sem.at[9], recv_sem.at[9], partner
            )
            inter_swap.start()
        mix = jnp.dot(
            coup[...], result, precision=lax.Precision.HIGHEST, preferred_element_type=F32
        )
        mix = mix.astype(BF16)
        mix_turned = (-sign[:norb] * swap(mix.astype(F32))).astype(BF16)

        def correct(j, carry, mix=mix, mix_turned=mix_turned):
            own = at(member * slab + j)
            other = at((1 - member) * slab + j)
            gain = dot(ini[0, at(j), :], mix_turned) + dot(ini[1, at(j), :], mix)
            field[own, :] = field[own, :] + time_step * gain
            gain = dot(other_ini[0, at(j), :], mix_turned) + dot(other_ini[1, at(j), :], mix)
            field[other, :] = field[other, :] + time_step * gain
            return carry

        lax.fori_loop(0, slab, correct, 0)

    weight = jnp.broadcast_to(occ[...], (8, norb))
    left_8 = lax.broadcasted_iota(jnp.int32, (8, norb), 1) < half
    keep_own = jnp.logical_xor(left_8, member == 1)
    weight = jnp.where(keep_own, weight, swap(weight))
    own_slot = 2 * dom + member
    lines = []
    for j in range(main):
        value = field[j * cells : (j + 1) * cells, :]
        line = lax.dot_general(
            weight,
            value * value,
            (((1,), (1,)), ((), ())),
            precision=lax.Precision.HIGHEST,
            preferred_element_type=F32,
        )
        lines.append(line[0:1])
    dens[own_slot] = jnp.concatenate(lines, axis=0)
    dens_sends = []
    for step in range(doms):
        for k in range(2):
            if step == 0 and k == 0:
                continue
            item = copy(
                dens.at[own_slot],
                dens.at[own_slot],
                dens_send.at[2 * step + k],
                dens_recv.at[own_slot],
                ((dom + step) % doms, 2 * pair + (member + k) % 2),
            )
            item.start()
            dens_sends.append(item)
    arrived(inter.at[1 - member], recv_sem.at[9])
    inter_out[0] = jnp.where(left[:norb], inter[0], swap(inter[1]))
    inter_out[1] = jnp.where(left[:norb], swap(inter[0]), inter[1])
    for step in range(doms):
        for k in range(2):
            if step == 0 and k == 0:
                continue
            slot = 2 * ((dom + step) % doms) + (member + k) % 2
            arrived(dens.at[slot], dens_recv.at[slot])

    own_density = jnp.zeros((main, cells), F32)
    lower_density = jnp.zeros((main, cells), F32)
    upper_density = jnp.zeros((main, cells), F32)
    lower_owner = neigh[dom, 0]
    upper_owner = neigh[dom, 1]
    lower_offset = offs[dom, 0]
    upper_offset = offs[dom, 1]
    for d in range(doms):
        full = dens[2 * d] + dens[2 * d + 1]
        own_density = jnp.where(dom == d, full, own_density)
        lower_density = jnp.where(lower_owner == d, full, lower_density)
        upper_density = jnp.where(upper_owner == d, full, upper_density)
    low = jnp.zeros((main, cells), F32)
    high = jnp.zeros((main, cells), F32)
    for o in range(rows_y - BUF + 1):
        shift = (cells - o * cols_z) % cells
        moved = pltpu.roll(lower_density, shift, 1) if shift else lower_density
        low = jnp.where(lower_offset == o, moved, low)
        shift = (cells - BUF * cols_z - o * cols_z) % cells
        moved = pltpu.roll(upper_density, shift, 1) if shift else upper_density
        high = jnp.where(upper_offset == o, moved, high)
    y_plane = lax.broadcasted_iota(jnp.int32, (main, cells), 1) // cols_z
    from_top = y_plane - (rows_y - BUF)
    weight_low = (y_plane.astype(F32) + 1.0) / (BUF + 1.0)
    weight_high = (BUF - from_top.astype(F32)) / (BUF + 1.0)
    blended = jnp.where(
        y_plane < BUF,
        own_density * weight_low + low * (1.0 - weight_low),
        jnp.where(
            from_top >= 0, own_density * weight_high + high * (1.0 - weight_high), own_density
        ),
    )
    external = jnp.concatenate([low_grid[slab:], high_grid[slab:]], axis=0)
    root = jnp.exp(jnp.log(blended + 1e-06) * (1.0 / 3.0))
    new_grid = external - xc_factor * root
    pot_out[...] = jnp.where(is_even, new_grid[:slab], new_grid[slab:])
    spread(half_step * new_grid, HALO)

    def finish_other(j, carry):
        plane = (1 - member) * slab + j
        rounded[at(plane), :] = phase(field[at(plane), :], HALO + plane).astype(BF16)
        return carry

    def finish_own(j, carry):
        plane = member * slab + j
        evolved[member, at(j), :] = phase(field[at(plane), :], HALO + plane).astype(BF16)
        return carry

    lax.fori_loop(0, slab, finish_other, 0)
    back = copy(
        rounded.at[other_rows], evolved.at[member], send_sem.at[10], recv_sem.at[10], partner
    )
    back.start()
    lax.fori_loop(0, slab, finish_own, 0)
    arrived(evolved.at[1 - member], recv_sem.at[10])

    def unpack(j, carry):
        zero = evolved[0, at(j), :].astype(F32)
        one = evolved[1, at(j), :].astype(F32)
        evolved_out[0, at(j), :] = jnp.where(left, zero, swap(one)).astype(BF16)
        evolved_out[1, at(j), :] = jnp.where(left, swap(zero), one).astype(BF16)
        return carry

    lax.fori_loop(0, slab, unpack, 0)

    @pl.when(has_outward)
    def _():
        for item in grid_edge + raw_edge:
            item.wait_send()

    @pl.when(has_lower)
    def _():
        edge_sends[0].wait_send()

    @pl.when(has_upper)
    def _():
        edge_sends[1].wait_send()

    for item in [grid_swap, raw_swap, ini_swap, inter_swap, back] + sum_sends + dens_sends:
        item.wait_send()


def shards(orbitals, initial, potential, external, occupation, coupling, neighbours, offsets):
    slab, rows_y, cols_z, norb = orbitals.shape[2:]
    doms = lax.axis_size("dom")
    space = lax.axis_size("space")
    cells = rows_y * cols_z
    rows = slab * cells
    main = 2 * slab
    total = main + 2 * HALO
    pairs = space // 2
    sizes = (doms, space, slab, rows_y, cols_z, norb)
    vmem = pl.BlockSpec(memory_space=pltpu.VMEM)
    smem = pl.BlockSpec(memory_space=pltpu.SMEM)
    dma = pltpu.SemaphoreType.DMA
    evolved, inter, new_grid = pl.pallas_call(
        functools.partial(body, sizes),
        out_shape=(
            jax.ShapeDtypeStruct((2, rows, norb), BF16),
            jax.ShapeDtypeStruct((2, norb, norb), F32),
            jax.ShapeDtypeStruct((slab, cells), F32),
        ),
        in_specs=[vmem] * 6 + [smem] * 2,
        out_specs=(vmem, vmem, vmem),
        scratch_shapes=[
            pltpu.VMEM((2, rows, norb), BF16),
            pltpu.VMEM((rows, norb), BF16),
            pltpu.VMEM((2, HALO * cells, norb), BF16),
            pltpu.VMEM((2, rows, norb), BF16),
            pltpu.VMEM((4, 2 * slab, cells), F32),
            pltpu.VMEM((STEPS, total * cells, norb), BF16),
            pltpu.VMEM((total * cells, norb), BF16),
            pltpu.VMEM((total * cells, norb), BF16),
            pltpu.VMEM((total * cells, norb), F32),
            pltpu.VMEM((total * cells, norb), F32),
            pltpu.VMEM((main * cells, norb), F32),
            pltpu.VMEM((main * cells, norb), F32),
            pltpu.VMEM((main * cells, norb), BF16),
            pltpu.VMEM((main * cells, norb), BF16),
            pltpu.VMEM((STEPS, pairs, norb, norb), BF16),
            pltpu.VMEM((2, norb, norb), F32),
            pltpu.VMEM((2 * doms, main, cells), F32),
            pltpu.VMEM((2, rows, norb), BF16),
            dma((11,)),
            dma((11,)),
            dma((STEPS, pairs)),
            dma((STEPS, pairs)),
            dma((2 * doms,)),
            dma((2 * doms,)),
        ],
        compiler_params=pltpu.CompilerParams(
            collective_id=0, has_side_effects=True, vmem_limit_bytes=32 * 1024 * 1024
        ),
    )(
        orbitals.reshape(2, rows, norb),
        initial.reshape(2, rows, norb),
        potential[0],
        external[0],
        occupation.reshape(1, norb),
        coupling,
        neighbours,
        offsets,
    )
    return (
        evolved.reshape(orbitals.shape),
        inter[None],
        new_grid[None],
    )


def solution(mesh):
    return jax.shard_map(
        shards,
        mesh=mesh,
        in_specs=(
            P("dom", None, "space", None, None, None),
            P("dom", None, "space", None, None, None),
            P("dom", "space", None),
            P("dom", "space", None),
            P(),
            P(),
            P(),
            P(),
        ),
        out_specs=(
            P("dom", None, "space", None, None, None),
            P("dom", None, None, None),
            P("dom", "space", None),
        ),
        check_vma=False,
    )
```

```python
import functools

import jax
import jax.numpy as jnp
from jax import lax
from jax.experimental import pallas as pl
from jax.experimental.pallas import tpu as pltpu
from jax.sharding import PartitionSpec as P

TAYLOR = 4
STEPS = 2
BUF = 4

time_step = 0.4
half_step = 0.2
xc_factor = 0.9847450218426965

F32 = jnp.float32
BF16 = jnp.bfloat16
HALO = TAYLOR


def body(
    sizes,
    orb_in,
    ini_in,
    pot_in,
    ext_in,
    occ_in,
    coup_in,
    neigh,
    offs,
    evolved_out,
    inter_out,
    pot_out,
    orb,
    ini,
    ext,
    occ,
    coup,
    packed,
    other_raw,
    halo_raw,
    other_ini,
    grids,
    source,
    term_a,
    term_b,
    term_c,
    cos_x,
    sin_x,
    field,
    odd,
    rounded,
    turned,
    sums,
    inter,
    dens,
    returned,
    load_sem,
    send_sem,
    recv_sem,
    sum_send,
    sum_recv,
    dens_send,
    dens_recv,
):
    doms, space, slab, rows_y, cols_z, norb = sizes
    cells = rows_y * cols_z
    pairs = space // 2
    half = norb // 2
    main = 2 * slab
    total = main + 2 * HALO
    rows = slab * cells
    edge = HALO * cells
    cells_total = space * rows

    dom = lax.axis_index("dom")
    place = lax.axis_index("space")
    pair = place // 2
    member = place % 2
    partner = (dom, 2 * pair + 1 - member)
    has_lower = pair > 0
    has_upper = pair < pairs - 1
    outward = pair + 2 * member - 1
    has_outward = jnp.logical_and(outward >= 0, outward < pairs)

    def copy(src, dst, ss, rs, device):
        return pltpu.make_async_remote_copy(
            src_ref=src,
            dst_ref=dst,
            send_sem=ss,
            recv_sem=rs,
            device_id=device,
            device_id_type=pl.DeviceIdType.MESH,
        )

    def arrived(dst, rs):
        copy(dst, dst, send_sem.at[0], rs, partner).wait_recv()

    loads = [
        pltpu.make_async_copy(src, dst, load_sem.at[k])
        for k, (src, dst) in enumerate(
            [
                (orb_in, orb),
                (pot_in, grids.at[0]),
                (ini_in, ini),
                (coup_in, coup),
                (ext_in, ext),
                (occ_in, occ),
            ]
        )
    ]
    for item in loads:
        item.start()
    barrier = pltpu.get_barrier_semaphore()

    def greet(device):
        pl.semaphore_signal(barrier, inc=1, device_id=device, device_id_type=pl.DeviceIdType.MESH)

    greet(partner)
    for step in range(1, pairs):
        greet((dom, 2 * ((pair + step) % pairs) + member))
    for step in range(1, doms):
        greet(((dom + step) % doms, 2 * pair))
        greet(((dom + step) % doms, 2 * pair + 1))

    @pl.when(has_outward)
    def _():
        greet((dom, 2 * outward + 1 - member))

    lane = lax.broadcasted_iota(jnp.int32, (cells, norb), 1)
    left = lane < half
    sign = jnp.where(left, -1.0, 1.0).astype(F32)

    def swap(value):
        return pltpu.roll(value, half, 1)

    def at(index, count=1):
        return pl.ds(pl.multiple_of(index * cells, cells), count * cells)

    def pack_plane(j, carry):
        re = orb[0, at(j), :].astype(F32)
        im = orb[1, at(j), :].astype(F32)
        packed[0, at(j), :] = jnp.where(left, re, swap(im)).astype(BF16)
        packed[1, at(j), :] = jnp.where(left, swap(re), im).astype(BF16)
        return carry

    loads[0].wait()
    lax.fori_loop(0, slab, pack_plane, 0)
    loads[1].wait()

    pl.semaphore_wait(barrier, pairs + 2 * (doms - 1) + has_outward.astype(jnp.int32))

    grid_swap = copy(grids.at[0], grids.at[1], send_sem.at[0], recv_sem.at[0], partner)
    grid_swap.start()
    role = 1 - member
    grid_edge = [
        copy(
            grids.at[0],
            grids.at[2 + role],
            send_sem.at[1 + k],
            recv_sem.at[1 + role],
            (dom, 2 * outward + k),
        )
        for k in range(2)
    ]
    first = pl.ds(pl.multiple_of(member * (rows - edge), cells), edge)
    raw_edge = [
        copy(
            packed.at[k, first],
            halo_raw.at[role],
            send_sem.at[3 + k],
            recv_sem.at[3 + role],
            (dom, 2 * outward + k),
        )
        for k in range(2)
    ]
    raw_swap = copy(packed.at[1 - member], other_raw, send_sem.at[5], recv_sem.at[5], partner)
    ini_swap = copy(ini, other_ini, send_sem.at[6], recv_sem.at[6], partner)

    raw_swap.start()

    @pl.when(has_outward)
    def _():
        for item in grid_edge + raw_edge:
            item.start()


    zero_edge = jnp.zeros((edge, norb), BF16)

    @pl.when(jnp.logical_not(has_lower))
    def _():
        grids[2] = jnp.zeros((slab, cells), F32)
        halo_raw[0] = zero_edge
        source[1, 0:edge, :] = zero_edge

    @pl.when(jnp.logical_not(has_upper))
    def _():
        grids[3] = jnp.zeros((slab, cells), F32)
        halo_raw[1] = zero_edge
        source[1, edge + main * cells :, :] = zero_edge

    def trig_table(angle):
        count = angle.shape[0]
        fill = jnp.zeros((norb - 2 * count, cells), F32)
        return jnp.concatenate([jnp.cos(angle), jnp.sin(angle), fill], axis=0).T

    def spread(angle):
        count = angle.shape[0]
        table = trig_table(angle)
        for j in range(count):
            here = slice(j * cells, (j + 1) * cells)
            cos_x[here, :] = jnp.broadcast_to(table[:, j : j + 1], (cells, norb))
            column = table[:, count + j : count + j + 1]
            sin_x[here, :] = jnp.broadcast_to(column, (cells, norb)) * sign

    arrived(grids.at[1], recv_sem.at[0])

    @pl.when(has_lower)
    def _():
        arrived(grids.at[2], recv_sem.at[1])

    @pl.when(has_upper)
    def _():
        arrived(grids.at[3], recv_sem.at[2])

    is_even = member == 0
    mine, theirs = grids[0], grids[1]
    spread(
        half_step
        * jnp.concatenate(
            [
                grids[2, slab - HALO : slab],
                jnp.where(is_even, mine, theirs),
                jnp.where(is_even, theirs, mine),
                grids[3, 0:HALO],
            ],
            axis=0,
        )
    )

    def phase(value, j):
        return cos_x[at(j), :] * value - sin_x[at(j), :] * swap(value)

    def begin(value, plane):
        value = phase(value.astype(F32), plane)
        field[at(plane), :] = value
        source[0, at(plane), :] = value.astype(BF16)

    def begin_own(j, carry):
        begin(packed[member, at(j), :], HALO + member * slab + j)
        return carry

    def begin_other(j, carry):
        begin(other_raw[at(j), :], HALO + (1 - member) * slab + j)
        return carry

    def begin_edges(j, carry):
        begin(halo_raw[0, at(j), :], j)
        begin(halo_raw[1, at(j), :], HALO + main + j)
        return carry

    lax.fori_loop(0, slab, begin_own, 0)
    arrived(other_raw, recv_sem.at[5])
    lax.fori_loop(0, slab, begin_other, 0)

    z_index = lax.broadcasted_iota(jnp.int32, (rows_y, cols_z, norb), 1)
    z_first = z_index == 0
    z_last = z_index == cols_z - 1
    zero_row = jnp.zeros((1, cols_z, norb), F32)
    lower_keep = has_lower.astype(F32)
    upper_keep = has_upper.astype(F32)

    def curvature(load, j):
        center = load(j).astype(F32).reshape(rows_y, cols_z, norb)
        outer = (load(j - 1).astype(F32) + load(j + 1).astype(F32)).reshape(center.shape)
        value = outer - 6.0 * center
        value = value + jnp.concatenate([center[1:], zero_row], axis=0)
        value = value + jnp.concatenate([zero_row, center[:-1]], axis=0)
        value = value + jnp.where(z_first, 0.0, pltpu.roll(center, 1, 1))
        value = value + jnp.where(z_last, 0.0, pltpu.roll(center, cols_z - 1, 1))
        return value.reshape(cells, norb)

    loads_of = [None, term_a, term_b, term_c]

    def update_of(section, order, j, keep=None):
        factor = time_step / (2.0 * order)
        if keep is not None:
            factor = factor * keep

        def load(plane):
            if order == 1:
                return source[section, at(plane), :]
            return loads_of[order - 1][at(plane), :]

        return factor * curvature(load, j)

    def add_term(order, j, update):
        here = at(j)
        loads_of[order][here, :] = update.astype(BF16)
        if order == 1:
            odd[here, :] = update
        elif order == 2:
            field[here, :] = field[here, :] - update
        else:
            odd[here, :] = odd[here, :] - update

    def add_last(j, update):
        here = at(j)
        value = field[here, :] + update + sign * swap(odd[here, :])
        value = phase(value, j)
        field[here, :] = value
        near = value.astype(BF16)
        rounded[at(j - HALO), :] = near
        turned[at(j - HALO), :] = (-sign * swap(near.astype(F32))).astype(BF16)

    def inner_terms(section):
        for order in range(1, TAYLOR):

            def pair_of_planes(i, carry, order=order):
                j, k = HALO + order + i, HALO + slab + i
                first_update = update_of(section, order, j)
                second_update = update_of(section, order, k)
                add_term(order, j, first_update)
                add_term(order, k, second_update)
                return carry

            if slab > order:
                lax.fori_loop(0, slab - order, pair_of_planes, 0)

    def outer_terms(section):
        for order in range(1, TAYLOR):

            def pair_of_planes(i, carry, order=order):
                j, k = order + i, HALO + main - order + i
                low_keep = jnp.where(j < HALO, lower_keep, 1.0)
                high_keep = jnp.where(k >= HALO + main, upper_keep, 1.0)
                first_update = update_of(section, order, j, low_keep)
                second_update = update_of(section, order, k, high_keep)
                add_term(order, j, first_update)
                add_term(order, k, second_update)
                return carry

            lax.fori_loop(0, HALO, pair_of_planes, 0)

        def last_pair(i, carry):
            j, k = HALO + i, HALO + slab + i
            first_update = update_of(section, TAYLOR, j)
            second_update = update_of(section, TAYLOR, k)
            add_last(j, first_update)
            add_last(k, second_update)
            return carry

        lax.fori_loop(0, slab, last_pair, 0)

    own_rows = pl.ds(pl.multiple_of(member * rows, cells), rows)
    other_rows = pl.ds(pl.multiple_of((1 - member) * rows, cells), rows)

    def contract(a, b):
        return lax.dot_general(a, b, (((0,), (0,)), ((), ())), preferred_element_type=F32)

    def dot(a, b):
        return jnp.dot(a, b, preferred_element_type=F32)

    def correction(section, initials, owner, mixes):
        chunk = 2 if slab % 2 == 0 else 1

        def planes(j, carry):
            from_rows = pl.ds(pl.multiple_of(j * chunk * cells, cells), chunk * cells)
            place_now = owner * slab + j * chunk
            both = jnp.concatenate([initials[0, from_rows, :], initials[1, from_rows, :]], axis=1)
            gain = time_step * dot(both, mixes)
            for k in range(chunk):
                plane = HALO + place_now + k
                value = field[at(plane), :] + gain[k * cells : (k + 1) * cells]
                if section < STEPS - 1:
                    value = phase(value, plane)
                    source[section + 1, at(plane), :] = value.astype(BF16)
                else:
                    rounded[at(plane - HALO), :] = value.astype(BF16)
                field[at(plane), :] = value
            return carry

        lax.fori_loop(0, slab // chunk, planes, 0)

    inward = pair + 1 - 2 * member
    has_inward = jnp.logical_and(inward >= 0, inward < pairs)

    def edge_send(owner, to, k, section):
        here = pl.multiple_of((HALO + owner * (main - HALO)) * cells, cells)
        there = pl.multiple_of((1 - owner) * (HALO + main) * cells, cells)
        return copy(
            source.at[section, pl.ds(here, edge)],
            source.at[section, pl.ds(there, edge)],
            send_sem.at[7 + k],
            recv_sem.at[8 - owner],
            (dom, 2 * to + member),
        )

    edge_out = edge_send(member, outward, 0, 1)
    edge_in = edge_send(1 - member, inward, 1, 1)
    sum_sends = []
    result = None
    for section in range(STEPS):
        inner_terms(section)
        if section == 0:

            @pl.when(has_lower)
            def _():
                arrived(halo_raw.at[0], recv_sem.at[3])

            @pl.when(has_upper)
            def _():
                arrived(halo_raw.at[1], recv_sem.at[4])

            loads[2].wait()
            ini_swap.start()
            lax.fori_loop(0, HALO, begin_edges, 0)
        else:

            @pl.when(has_lower)
            def _():
                arrived(source.at[1, pl.ds(0, edge)], recv_sem.at[7])

            @pl.when(has_upper)
            def _():
                arrived(source.at[1, pl.ds(edge + main * cells, edge)], recv_sem.at[8])

        outer_terms(section)
        part = contract(ini[0], rounded[own_rows, :]) + contract(ini[1], turned[own_rows, :])
        if section == 0:
            arrived(other_ini, recv_sem.at[6])
            loads[3].wait()
        part = part + contract(other_ini[0], rounded[other_rows, :])
        part = part + contract(other_ini[1], turned[other_rows, :])
        sums[section, pair] = (part * (1.0 / cells_total)).astype(sums.dtype)
        for step in range(1, pairs):
            item = copy(
                sums.at[section, pair],
                sums.at[section, pair],
                sum_send.at[section, step],
                sum_recv.at[section, pair],
                (dom, 2 * ((pair + step) % pairs) + member),
            )
            item.start()
            sum_sends.append(item)
        for step in range(1, pairs):
            slot = (pair + step) % pairs
            arrived(sums.at[section, slot], sum_recv.at[section, slot])
        result = sums[section, 0].astype(F32)
        for slot in range(1, pairs):
            result = result + sums[section, slot].astype(F32)
        mix = jnp.dot(
            coup[...], result, precision=lax.Precision.HIGHEST, preferred_element_type=F32
        )
        mix = mix.astype(BF16)
        mix_turned = (-sign[:norb] * swap(mix.astype(F32))).astype(BF16)
        mixes = jnp.concatenate([mix_turned, mix], axis=0)
        correction(section, ini, member, mixes)
        if section < STEPS - 1:

            @pl.when(has_outward)
            def _():
                edge_out.start()

        correction(section, other_ini, 1 - member, mixes)
        if section < STEPS - 1:

            @pl.when(has_inward)
            def _():
                edge_in.start()

    loads[4].wait()
    loads[5].wait()
    weight = jnp.broadcast_to(occ[...], (8, norb))
    left_8 = lax.broadcasted_iota(jnp.int32, (8, norb), 1) < half
    keep_own = jnp.logical_xor(left_8, member == 1)
    weight = jnp.where(keep_own, weight, swap(weight))[0:1]
    own_slot = 2 * dom + member
    lines = []
    for j in range(main):
        value = field[(HALO + j) * cells : (HALO + j + 1) * cells, :]
        lines.append(jnp.sum((value * value * weight).T, axis=0, keepdims=True))
    dens[own_slot] = jnp.concatenate(lines, axis=0)
    dens_sends = []
    for step in range(doms):
        for k in range(2):
            if step == 0 and k == 0:
                continue
            item = copy(
                dens.at[own_slot],
                dens.at[own_slot],
                dens_send.at[2 * step + k],
                dens_recv.at[own_slot],
                ((dom + step) % doms, 2 * pair + (member + k) % 2),
            )
            item.start()
            dens_sends.append(item)
    back = copy(rounded.at[other_rows], returned, send_sem.at[10], recv_sem.at[10], partner)
    back.start()
    inter[member] = result
    inter_swap = copy(
        inter.at[member], inter.at[member], send_sem.at[9], recv_sem.at[9], partner
    )
    inter_swap.start()
    for step in range(doms):
        for k in range(2):
            if step == 0 and k == 0:
                continue
            slot = 2 * ((dom + step) % doms) + (member + k) % 2
            arrived(dens.at[slot], dens_recv.at[slot])

    own_density = jnp.zeros((main, cells), F32)
    lower_density = jnp.zeros((main, cells), F32)
    upper_density = jnp.zeros((main, cells), F32)
    lower_owner = neigh[0, dom]
    upper_owner = neigh[1, dom]
    lower_offset = offs[0, dom]
    upper_offset = offs[1, dom]
    for d in range(doms):
        full = dens[2 * d] + dens[2 * d + 1]
        own_density = jnp.where(dom == d, full, own_density)
        lower_density = jnp.where(lower_owner == d, full, lower_density)
        upper_density = jnp.where(upper_owner == d, full, upper_density)
    low = jnp.zeros((main, cells), F32)
    high = jnp.zeros((main, cells), F32)
    for o in range(rows_y - BUF + 1):
        shift = (cells - o * cols_z) % cells
        moved = pltpu.roll(lower_density, shift, 1) if shift else lower_density
        low = jnp.where(lower_offset == o, moved, low)
        shift = (cells - BUF * cols_z - o * cols_z) % cells
        moved = pltpu.roll(upper_density, shift, 1) if shift else upper_density
        high = jnp.where(upper_offset == o, moved, high)
    y_plane = lax.broadcasted_iota(jnp.int32, (main, cells), 1) // cols_z
    from_top = y_plane - (rows_y - BUF)
    weight_low = (y_plane.astype(F32) + 1.0) / (BUF + 1.0)
    weight_high = (BUF - from_top.astype(F32)) / (BUF + 1.0)
    blended = jnp.where(
        y_plane < BUF,
        own_density * weight_low + low * (1.0 - weight_low),
        jnp.where(
            from_top >= 0, own_density * weight_high + high * (1.0 - weight_high), own_density
        ),
    )
    blended = jnp.where(is_even, blended[:slab], blended[slab:])
    root = jnp.exp(jnp.log(blended + 1e-06) * (1.0 / 3.0))
    new_grid = ext[...] - xc_factor * root
    pot_out[...] = new_grid
    table = trig_table(half_step * new_grid)
    arrived(returned, recv_sem.at[10])

    for j in range(slab):
        here = slice(j * cells, (j + 1) * cells)
        cos_v = table[:, j : j + 1]
        sin_v = table[:, slab + j : slab + j + 1]
        own_half = field[at(HALO + member * slab + j), :]
        other_half = returned[here, :].astype(F32)
        zero = jnp.where(is_even, own_half, other_half)
        one = jnp.where(is_even, other_half, own_half)
        re = jnp.where(left, zero, swap(one))
        im = jnp.where(left, swap(zero), one)
        evolved_out[0, here, :] = (cos_v * re + sin_v * im).astype(BF16)
        evolved_out[1, here, :] = (cos_v * im - sin_v * re).astype(BF16)
    arrived(inter.at[1 - member], recv_sem.at[9])
    inter_out[0] = jnp.where(left[:norb], inter[0], swap(inter[1]))
    inter_out[1] = jnp.where(left[:norb], swap(inter[0]), inter[1])

    @pl.when(has_outward)
    def _():
        for item in grid_edge + raw_edge:
            item.wait_send()

    @pl.when(has_outward)
    def _():
        edge_out.wait_send()

    @pl.when(has_inward)
    def _():
        edge_in.wait_send()

    for item in [grid_swap, raw_swap, ini_swap, inter_swap, back] + sum_sends + dens_sends:
        item.wait_send()


def shards(orbitals, initial, potential, external, occupation, coupling, neighbours, offsets):
    slab, rows_y, cols_z, norb = orbitals.shape[2:]
    doms = lax.axis_size("dom")
    space = lax.axis_size("space")
    cells = rows_y * cols_z
    rows = slab * cells
    main = 2 * slab
    total = main + 2 * HALO
    pairs = space // 2
    sizes = (doms, space, slab, rows_y, cols_z, norb)
    vmem = pl.BlockSpec(memory_space=pltpu.VMEM)
    hbm = pl.BlockSpec(memory_space=pltpu.HBM)
    smem = pl.BlockSpec(memory_space=pltpu.SMEM)
    dma = pltpu.SemaphoreType.DMA
    evolved, inter, new_grid = pl.pallas_call(
        functools.partial(body, sizes),
        out_shape=(
            jax.ShapeDtypeStruct((2, rows, norb), BF16),
            jax.ShapeDtypeStruct((2, norb, norb), F32),
            jax.ShapeDtypeStruct((slab, cells), F32),
        ),
        in_specs=[hbm] * 6 + [smem] * 2,
        out_specs=(vmem, vmem, vmem),
        scratch_shapes=[
            pltpu.VMEM((2, rows, norb), BF16),
            pltpu.VMEM((2, rows, norb), BF16),
            pltpu.VMEM((slab, cells), F32),
            pltpu.VMEM((1, norb), F32),
            pltpu.VMEM((norb, norb), F32),
            pltpu.VMEM((2, rows, norb), BF16),
            pltpu.VMEM((rows, norb), BF16),
            pltpu.VMEM((2, HALO * cells, norb), BF16),
            pltpu.VMEM((2, rows, norb), BF16),
            pltpu.VMEM((4, slab, cells), F32),
            pltpu.VMEM((STEPS, total * cells, norb), BF16),
            pltpu.VMEM((total * cells, norb), BF16),
            pltpu.VMEM((total * cells, norb), BF16),
            pltpu.VMEM((total * cells, norb), BF16),
            pltpu.VMEM((total * cells, norb), F32),
            pltpu.VMEM((total * cells, norb), F32),
            pltpu.VMEM((total * cells, norb), F32),
            pltpu.VMEM((total * cells, norb), F32),
            pltpu.VMEM((main * cells, norb), BF16),
            pltpu.VMEM((main * cells, norb), BF16),
            pltpu.VMEM((STEPS, pairs, norb, norb), BF16),
            pltpu.VMEM((2, norb, norb), F32),
            pltpu.VMEM((2 * doms, main, cells), F32),
            pltpu.VMEM((rows, norb), BF16),
            dma((6,)),
            dma((11,)),
            dma((11,)),
            dma((STEPS, pairs)),
            dma((STEPS, pairs)),
            dma((2 * doms,)),
            dma((2 * doms,)),
        ],
        compiler_params=pltpu.CompilerParams(
            collective_id=0, has_side_effects=True, vmem_limit_bytes=32 * 1024 * 1024
        ),
    )(
        orbitals.reshape(2, rows, norb),
        initial.reshape(2, rows, norb),
        potential[0],
        external[0],
        occupation.reshape(1, norb),
        coupling,
        neighbours.T,
        offsets.T,
    )
    return (
        evolved.reshape(orbitals.shape),
        inter[None],
        new_grid[None],
    )


def solution(mesh):
    return jax.shard_map(
        shards,
        mesh=mesh,
        in_specs=(
            P("dom", None, "space", None, None, None),
            P("dom", None, "space", None, None, None),
            P("dom", "space", None),
            P("dom", "space", None),
            P(),
            P(),
            P(),
            P(),
        ),
        out_specs=(
            P("dom", None, "space", None, None, None),
            P("dom", None, None, None),
            P("dom", "space", None),
        ),
        check_vma=False,
    )
```

```python
import functools

import jax
import jax.numpy as jnp
from jax import lax
from jax.experimental import pallas as pl
from jax.experimental.pallas import tpu as pltpu
from jax.sharding import PartitionSpec as P

TAYLOR = 4
STEPS = 2
BUF = 4

time_step = 0.4
half_step = 0.2
xc_factor = 0.9847450218426965

F32 = jnp.float32
BF16 = jnp.bfloat16
HALO = TAYLOR


def body(
    sizes,
    orb_in,
    ini_in,
    pot_in,
    ext_in,
    occ_in,
    coup_in,
    neigh,
    offs,
    evolved_out,
    inter_out,
    pot_out,
    orb,
    ini,
    ext,
    occ,
    coup,
    packed,
    other_raw,
    halo_raw,
    other_ini,
    grids,
    source,
    term_a,
    term_b,
    term_c,
    cos_x,
    sin_x,
    field,
    odd,
    rounded,
    turned,
    sums,
    inter,
    dens,
    returned,
    load_sem,
    send_sem,
    recv_sem,
    sum_send,
    sum_recv,
    dens_send,
    dens_recv,
    swap_send,
    swap_recv,
    edge_send_sem,
    edge_recv_sem,
):
    doms, space, slab, rows_y, cols_z, norb = sizes
    cells = rows_y * cols_z
    pairs = space // 2
    half = norb // 2
    main = 2 * slab
    total = main + 2 * HALO
    rows = slab * cells
    edge = HALO * cells
    cells_total = space * rows

    dom = lax.axis_index("dom")
    place = lax.axis_index("space")
    pair = place // 2
    member = place % 2
    partner = (dom, 2 * pair + 1 - member)
    has_lower = pair > 0
    has_upper = pair < pairs - 1
    outward = pair + 2 * member - 1
    has_outward = jnp.logical_and(outward >= 0, outward < pairs)
    inward = pair + 1 - 2 * member
    has_inward = jnp.logical_and(inward >= 0, inward < pairs)
    chunks = 2 if slab == HALO and slab % 2 == 0 else 1

    def copy(src, dst, ss, rs, device):
        return pltpu.make_async_remote_copy(
            src_ref=src,
            dst_ref=dst,
            send_sem=ss,
            recv_sem=rs,
            device_id=device,
            device_id_type=pl.DeviceIdType.MESH,
        )

    def arrived(dst, rs):
        copy(dst, dst, send_sem.at[0], rs, partner).wait_recv()

    loads = [
        pltpu.make_async_copy(src, dst, load_sem.at[k])
        for k, (src, dst) in enumerate(
            [
                (orb_in, orb),
                (pot_in, grids.at[0]),
                (ini_in, ini),
                (coup_in, coup),
                (ext_in, ext),
                (occ_in, occ),
            ]
        )
    ]
    for item in loads:
        item.start()
    barrier = pltpu.get_barrier_semaphore()

    def greet(device):
        pl.semaphore_signal(barrier, inc=1, device_id=device, device_id_type=pl.DeviceIdType.MESH)

    greet(partner)
    for step in range(1, pairs):
        greet((dom, 2 * ((pair + step) % pairs) + member))
    for step in range(1, doms):
        greet(((dom + step) % doms, 2 * pair))
        greet(((dom + step) % doms, 2 * pair + 1))

    lane = lax.broadcasted_iota(jnp.int32, (cells, norb), 1)
    left = lane < half
    sign = jnp.where(left, -1.0, 1.0).astype(F32)

    def swap(value):
        return pltpu.roll(value, half, 1)

    def at(index, count=1):
        return pl.ds(pl.multiple_of(index * cells, cells), count * cells)

    def pack_plane(j, carry):
        re = orb[0, at(j), :].astype(F32)
        im = orb[1, at(j), :].astype(F32)
        packed[0, at(j), :] = jnp.where(left, re, swap(im)).astype(BF16)
        packed[1, at(j), :] = jnp.where(left, swap(re), im).astype(BF16)
        return carry

    loads[0].wait()
    lax.fori_loop(0, slab, pack_plane, 0)
    loads[1].wait()

    pl.semaphore_wait(barrier, pairs + 2 * (doms - 1))

    grid_swap = copy(grids.at[0], grids.at[1], send_sem.at[0], recv_sem.at[0], partner)
    grid_swap.start()
    role = 1 - member
    onward = (dom, 2 * outward + member)
    back_in = (dom, 2 * inward + member)
    grid_edge = copy(
        grids.at[0], grids.at[2 + role], send_sem.at[1], recv_sem.at[1 + role], onward
    )
    grid_forward = copy(
        grids.at[1], grids.at[2 + member], send_sem.at[2], recv_sem.at[1 + member], back_in
    )
    swap_rows = rows // chunks
    edge_rows = edge // chunks

    def span(c, length):
        return pl.ds(c * length, length)

    def edge_span(owner, c):
        start = owner * (rows - edge) + c * edge_rows
        return pl.ds(pl.multiple_of(start, cells), edge_rows)

    raw_swap = [
        copy(
            packed.at[1 - member, span(c, swap_rows)],
            other_raw.at[span(c, swap_rows)],
            swap_send.at[c],
            swap_recv.at[c],
            partner,
        )
        for c in range(chunks)
    ]
    raw_edge = [
        copy(
            packed.at[member, edge_span(member, c)],
            halo_raw.at[role, span(c, edge_rows)],
            edge_send_sem.at[0, c],
            edge_recv_sem.at[role, c],
            onward,
        )
        for c in range(chunks)
    ]
    raw_forward = [
        copy(
            other_raw.at[edge_span(1 - member, c)],
            halo_raw.at[member, span(c, edge_rows)],
            edge_send_sem.at[1, c],
            edge_recv_sem.at[member, c],
            back_in,
        )
        for c in range(chunks)
    ]
    ini_swap = copy(ini, other_ini, send_sem.at[6], recv_sem.at[6], partner)
    for item in raw_swap:
        item.start()

    @pl.when(has_outward)
    def _():
        grid_edge.start()
        for item in raw_edge:
            item.start()

    zero_edge = jnp.zeros((edge, norb), BF16)

    @pl.when(jnp.logical_not(has_lower))
    def _():
        grids[2] = jnp.zeros((slab, cells), F32)
        halo_raw[0] = zero_edge
        source[1, 0:edge, :] = zero_edge

    @pl.when(jnp.logical_not(has_upper))
    def _():
        grids[3] = jnp.zeros((slab, cells), F32)
        halo_raw[1] = zero_edge
        source[1, edge + main * cells :, :] = zero_edge

    def trig_table(angle):
        count = angle.shape[0]
        fill = jnp.zeros((norb - 2 * count, cells), F32)
        return jnp.concatenate([jnp.cos(angle), jnp.sin(angle), fill], axis=0).T

    def spread(angle, planes):
        count = angle.shape[0]
        table = trig_table(angle)
        for j, plane in enumerate(planes):
            here = slice(plane * cells, (plane + 1) * cells)
            cos_x[here, :] = jnp.broadcast_to(table[:, j : j + 1], (cells, norb))
            column = table[:, count + j : count + j + 1]
            sin_x[here, :] = jnp.broadcast_to(column, (cells, norb)) * sign

    arrived(grids.at[1], recv_sem.at[0])

    @pl.when(has_inward)
    def _():
        grid_forward.start()

    is_even = member == 0
    mine, theirs = grids[0], grids[1]
    both_grids = [jnp.where(is_even, mine, theirs), jnp.where(is_even, theirs, mine)]
    spread(half_step * jnp.concatenate(both_grids, axis=0), range(HALO, HALO + main))

    def phase(value, j):
        return cos_x[at(j), :] * value - sin_x[at(j), :] * swap(value)

    def begin(value, plane):
        value = phase(value.astype(F32), plane)
        field[at(plane), :] = value
        source[0, at(plane), :] = value.astype(BF16)

    def begin_own(j, carry):
        begin(packed[member, at(j), :], HALO + member * slab + j)
        return carry

    def begin_other(j, carry):
        begin(other_raw[at(j), :], HALO + (1 - member) * slab + j)
        return carry

    def begin_edges(j, carry):
        begin(halo_raw[0, at(j), :], j)
        begin(halo_raw[1, at(j), :], HALO + main + j)
        return carry

    lax.fori_loop(0, slab, begin_own, 0)
    for c in range(chunks):
        arrived(other_raw.at[span(c, swap_rows)], swap_recv.at[c])

        @pl.when(has_inward)
        def _():
            raw_forward[c].start()

        if c == 0:
            loads[2].wait()
            ini_swap.start()
        lax.fori_loop(c * (slab // chunks), (c + 1) * (slab // chunks), begin_other, 0)

    z_index = lax.broadcasted_iota(jnp.int32, (rows_y, cols_z, norb), 1)
    z_first = z_index == 0
    z_last = z_index == cols_z - 1
    zero_row = jnp.zeros((1, cols_z, norb), F32)
    lower_keep = has_lower.astype(F32)
    upper_keep = has_upper.astype(F32)

    def curvature(load, j):
        center = load(j).astype(F32).reshape(rows_y, cols_z, norb)
        outer = (load(j - 1).astype(F32) + load(j + 1).astype(F32)).reshape(center.shape)
        value = outer - 6.0 * center
        value = value + jnp.concatenate([center[1:], zero_row], axis=0)
        value = value + jnp.concatenate([zero_row, center[:-1]], axis=0)
        value = value + jnp.where(z_first, 0.0, pltpu.roll(center, 1, 1))
        value = value + jnp.where(z_last, 0.0, pltpu.roll(center, cols_z - 1, 1))
        return value.reshape(cells, norb)

    loads_of = [None, term_a, term_b, term_c]

    def update_of(section, order, j, keep=None):
        factor = time_step / (2.0 * order)
        if keep is not None:
            factor = factor * keep

        def load(plane):
            if order == 1:
                return source[section, at(plane), :]
            return loads_of[order - 1][at(plane), :]

        return factor * curvature(load, j)

    def add_term(order, j, update):
        here = at(j)
        loads_of[order][here, :] = update.astype(BF16)
        if order == 1:
            odd[here, :] = update
        elif order == 2:
            field[here, :] = field[here, :] - update
        else:
            odd[here, :] = odd[here, :] - update

    def add_last(j, update):
        here = at(j)
        value = field[here, :] + update + sign * swap(odd[here, :])
        value = phase(value, j)
        field[here, :] = value
        near = value.astype(BF16)
        rounded[at(j - HALO), :] = near
        turned[at(j - HALO), :] = (-sign * swap(near.astype(F32))).astype(BF16)

    def inner_terms(section):
        for order in range(1, TAYLOR):

            def pair_of_planes(i, carry, order=order):
                j, k = HALO + order + i, HALO + slab + i
                first_update = update_of(section, order, j)
                second_update = update_of(section, order, k)
                add_term(order, j, first_update)
                add_term(order, k, second_update)
                return carry

            if slab > order:
                lax.fori_loop(0, slab - order, pair_of_planes, 0)

    def outer_terms(section):
        for order in range(1, TAYLOR):

            def pair_of_planes(i, carry, order=order):
                j, k = order + i, HALO + main - order + i
                low_keep = jnp.where(j < HALO, lower_keep, 1.0)
                high_keep = jnp.where(k >= HALO + main, upper_keep, 1.0)
                first_update = update_of(section, order, j, low_keep)
                second_update = update_of(section, order, k, high_keep)
                add_term(order, j, first_update)
                add_term(order, k, second_update)
                return carry

            lax.fori_loop(0, HALO, pair_of_planes, 0)

        def last_pair(i, carry):
            j, k = HALO + i, HALO + slab + i
            first_update = update_of(section, TAYLOR, j)
            second_update = update_of(section, TAYLOR, k)
            add_last(j, first_update)
            add_last(k, second_update)
            return carry

        lax.fori_loop(0, slab, last_pair, 0)

    own_rows = pl.ds(pl.multiple_of(member * rows, cells), rows)
    other_rows = pl.ds(pl.multiple_of((1 - member) * rows, cells), rows)

    def contract(a, b):
        return lax.dot_general(a, b, (((0,), (0,)), ((), ())), preferred_element_type=F32)

    def dot(a, b):
        return jnp.dot(a, b, preferred_element_type=F32)

    def correction(section, initials, owner, mixes):
        chunk = 2 if slab % 2 == 0 else 1

        def planes(j, carry):
            from_rows = pl.ds(pl.multiple_of(j * chunk * cells, cells), chunk * cells)
            place_now = owner * slab + j * chunk
            both = jnp.concatenate([initials[0, from_rows, :], initials[1, from_rows, :]], axis=1)
            gain = time_step * dot(both, mixes)
            for k in range(chunk):
                plane = HALO + place_now + k
                value = field[at(plane), :] + gain[k * cells : (k + 1) * cells]
                if section < STEPS - 1:
                    value = phase(value, plane)
                    source[section + 1, at(plane), :] = value.astype(BF16)
                else:
                    rounded[at(plane - HALO), :] = value.astype(BF16)
                field[at(plane), :] = value
            return carry

        lax.fori_loop(0, slab // chunk, planes, 0)

    def edge_send(owner, to, k, section):
        here = pl.multiple_of((HALO + owner * (main - HALO)) * cells, cells)
        there = pl.multiple_of((1 - owner) * (HALO + main) * cells, cells)
        return copy(
            source.at[section, pl.ds(here, edge)],
            source.at[section, pl.ds(there, edge)],
            send_sem.at[7 + k],
            recv_sem.at[8 - owner],
            (dom, 2 * to + member),
        )

    edge_out = edge_send(member, outward, 0, 1)
    edge_in = edge_send(1 - member, inward, 1, 1)
    sum_sends = []
    result = None
    for section in range(STEPS):
        inner_terms(section)
        if section == 0:

            @pl.when(has_lower)
            def _():
                arrived(grids.at[2], recv_sem.at[1])

            @pl.when(has_upper)
            def _():
                arrived(grids.at[3], recv_sem.at[2])

            ends = jnp.concatenate([grids[2, slab - HALO : slab], grids[3, 0:HALO]], axis=0)
            spread(half_step * ends, [*range(HALO), *range(HALO + main, total)])

            @pl.when(has_lower)
            def _():
                for c in range(chunks):
                    arrived(halo_raw.at[0, span(c, edge_rows)], edge_recv_sem.at[0, c])

            @pl.when(has_upper)
            def _():
                for c in range(chunks):
                    arrived(halo_raw.at[1, span(c, edge_rows)], edge_recv_sem.at[1, c])

            lax.fori_loop(0, HALO, begin_edges, 0)
        else:

            @pl.when(has_lower)
            def _():
                arrived(source.at[1, pl.ds(0, edge)], recv_sem.at[7])

            @pl.when(has_upper)
            def _():
                arrived(source.at[1, pl.ds(edge + main * cells, edge)], recv_sem.at[8])

        outer_terms(section)
        part = contract(ini[0], rounded[own_rows, :]) + contract(ini[1], turned[own_rows, :])
        if section == 0:
            arrived(other_ini, recv_sem.at[6])
            loads[3].wait()
        part = part + contract(other_ini[0], rounded[other_rows, :])
        part = part + contract(other_ini[1], turned[other_rows, :])
        sums[section, pair] = (part * (1.0 / cells_total)).astype(sums.dtype)
        for step in range(1, pairs):
            item = copy(
                sums.at[section, pair],
                sums.at[section, pair],
                sum_send.at[section, step],
                sum_recv.at[section, pair],
                (dom, 2 * ((pair + step) % pairs) + member),
            )
            item.start()
            sum_sends.append(item)
        for step in range(1, pairs):
            slot = (pair + step) % pairs
            arrived(sums.at[section, slot], sum_recv.at[section, slot])
        result = sums[section, 0].astype(F32)
        for slot in range(1, pairs):
            result = result + sums[section, slot].astype(F32)
        mix = jnp.dot(
            coup[...], result, precision=lax.Precision.HIGHEST, preferred_element_type=F32
        )
        mix = mix.astype(BF16)
        mix_turned = (-sign[:norb] * swap(mix.astype(F32))).astype(BF16)
        mixes = jnp.concatenate([mix_turned, mix], axis=0)
        correction(section, ini, member, mixes)
        if section < STEPS - 1:

            @pl.when(has_outward)
            def _():
                edge_out.start()

        correction(section, other_ini, 1 - member, mixes)
        if section < STEPS - 1:

            @pl.when(has_inward)
            def _():
                edge_in.start()

    loads[4].wait()
    loads[5].wait()
    weight = jnp.broadcast_to(occ[...], (8, norb))
    left_8 = lax.broadcasted_iota(jnp.int32, (8, norb), 1) < half
    keep_own = jnp.logical_xor(left_8, member == 1)
    weight = jnp.where(keep_own, weight, swap(weight))[0:1]
    own_slot = 2 * dom + member
    lines = []
    for j in range(main):
        value = field[(HALO + j) * cells : (HALO + j + 1) * cells, :]
        lines.append(jnp.sum((value * value * weight).T, axis=0, keepdims=True))
    dens[own_slot] = jnp.concatenate(lines, axis=0)
    dens_sends = []
    for step in range(doms):
        for k in range(2):
            if step == 0 and k == 0:
                continue
            item = copy(
                dens.at[own_slot],
                dens.at[own_slot],
                dens_send.at[2 * step + k],
                dens_recv.at[own_slot],
                ((dom + step) % doms, 2 * pair + (member + k) % 2),
            )
            item.start()
            dens_sends.append(item)
    back = copy(rounded.at[other_rows], returned, send_sem.at[10], recv_sem.at[10], partner)
    back.start()
    inter[member] = result
    inter_swap = copy(
        inter.at[member], inter.at[member], send_sem.at[9], recv_sem.at[9], partner
    )
    inter_swap.start()
    for step in range(doms):
        for k in range(2):
            if step == 0 and k == 0:
                continue
            slot = 2 * ((dom + step) % doms) + (member + k) % 2
            arrived(dens.at[slot], dens_recv.at[slot])

    own_density = jnp.zeros((main, cells), F32)
    lower_density = jnp.zeros((main, cells), F32)
    upper_density = jnp.zeros((main, cells), F32)
    lower_owner = neigh[0, dom]
    upper_owner = neigh[1, dom]
    lower_offset = offs[0, dom]
    upper_offset = offs[1, dom]
    for d in range(doms):
        full = dens[2 * d] + dens[2 * d + 1]
        own_density = jnp.where(dom == d, full, own_density)
        lower_density = jnp.where(lower_owner == d, full, lower_density)
        upper_density = jnp.where(upper_owner == d, full, upper_density)
    low = jnp.zeros((main, cells), F32)
    high = jnp.zeros((main, cells), F32)
    for o in range(rows_y - BUF + 1):
        shift = (cells - o * cols_z) % cells
        moved = pltpu.roll(lower_density, shift, 1) if shift else lower_density
        low = jnp.where(lower_offset == o, moved, low)
        shift = (cells - BUF * cols_z - o * cols_z) % cells
        moved = pltpu.roll(upper_density, shift, 1) if shift else upper_density
        high = jnp.where(upper_offset == o, moved, high)
    y_plane = lax.broadcasted_iota(jnp.int32, (main, cells), 1) // cols_z
    from_top = y_plane - (rows_y - BUF)
    weight_low = (y_plane.astype(F32) + 1.0) / (BUF + 1.0)
    weight_high = (BUF - from_top.astype(F32)) / (BUF + 1.0)
    blended = jnp.where(
        y_plane < BUF,
        own_density * weight_low + low * (1.0 - weight_low),
        jnp.where(
            from_top >= 0, own_density * weight_high + high * (1.0 - weight_high), own_density
        ),
    )
    blended = jnp.where(is_even, blended[:slab], blended[slab:])
    root = jnp.exp(jnp.log(blended + 1e-06) * (1.0 / 3.0))
    new_grid = ext[...] - xc_factor * root
    pot_out[...] = new_grid
    table = trig_table(half_step * new_grid)
    arrived(returned, recv_sem.at[10])

    for j in range(slab):
        here = slice(j * cells, (j + 1) * cells)
        cos_v = table[:, j : j + 1]
        sin_v = table[:, slab + j : slab + j + 1]
        own_half = field[at(HALO + member * slab + j), :]
        other_half = returned[here, :].astype(F32)
        zero = jnp.where(is_even, own_half, other_half)
        one = jnp.where(is_even, other_half, own_half)
        re = jnp.where(left, zero, swap(one))
        im = jnp.where(left, swap(zero), one)
        evolved_out[0, here, :] = (cos_v * re + sin_v * im).astype(BF16)
        evolved_out[1, here, :] = (cos_v * im - sin_v * re).astype(BF16)
    arrived(inter.at[1 - member], recv_sem.at[9])
    inter_out[0] = jnp.where(left[:norb], inter[0], swap(inter[1]))
    inter_out[1] = jnp.where(left[:norb], swap(inter[0]), inter[1])

    @pl.when(has_outward)
    def _():
        for item in [grid_edge] + raw_edge:
            item.wait_send()

    @pl.when(has_outward)
    def _():
        edge_out.wait_send()

    @pl.when(has_inward)
    def _():
        edge_in.wait_send()
        for item in [grid_forward] + raw_forward:
            item.wait_send()

    for item in [grid_swap, ini_swap, inter_swap, back] + raw_swap + sum_sends + dens_sends:
        item.wait_send()


def shards(orbitals, initial, potential, external, occupation, coupling, neighbours, offsets):
    slab, rows_y, cols_z, norb = orbitals.shape[2:]
    doms = lax.axis_size("dom")
    space = lax.axis_size("space")
    cells = rows_y * cols_z
    rows = slab * cells
    main = 2 * slab
    total = main + 2 * HALO
    pairs = space // 2
    sizes = (doms, space, slab, rows_y, cols_z, norb)
    vmem = pl.BlockSpec(memory_space=pltpu.VMEM)
    hbm = pl.BlockSpec(memory_space=pltpu.HBM)
    smem = pl.BlockSpec(memory_space=pltpu.SMEM)
    dma = pltpu.SemaphoreType.DMA
    evolved, inter, new_grid = pl.pallas_call(
        functools.partial(body, sizes),
        out_shape=(
            jax.ShapeDtypeStruct((2, rows, norb), BF16),
            jax.ShapeDtypeStruct((2, norb, norb), F32),
            jax.ShapeDtypeStruct((slab, cells), F32),
        ),
        in_specs=[hbm] * 6 + [smem] * 2,
        out_specs=(vmem, vmem, vmem),
        scratch_shapes=[
            pltpu.VMEM((2, rows, norb), BF16),
            pltpu.VMEM((2, rows, norb), BF16),
            pltpu.VMEM((slab, cells), F32),
            pltpu.VMEM((1, norb), F32),
            pltpu.VMEM((norb, norb), F32),
            pltpu.VMEM((2, rows, norb), BF16),
            pltpu.VMEM((rows, norb), BF16),
            pltpu.VMEM((2, HALO * cells, norb), BF16),
            pltpu.VMEM((2, rows, norb), BF16),
            pltpu.VMEM((4, slab, cells), F32),
            pltpu.VMEM((STEPS, total * cells, norb), BF16),
            pltpu.VMEM((total * cells, norb), BF16),
            pltpu.VMEM((total * cells, norb), BF16),
            pltpu.VMEM((total * cells, norb), BF16),
            pltpu.VMEM((total * cells, norb), F32),
            pltpu.VMEM((total * cells, norb), F32),
            pltpu.VMEM((total * cells, norb), F32),
            pltpu.VMEM((total * cells, norb), F32),
            pltpu.VMEM((main * cells, norb), BF16),
            pltpu.VMEM((main * cells, norb), BF16),
            pltpu.VMEM((STEPS, pairs, norb, norb), BF16),
            pltpu.VMEM((2, norb, norb), F32),
            pltpu.VMEM((2 * doms, main, cells), F32),
            pltpu.VMEM((rows, norb), BF16),
            dma((6,)),
            dma((11,)),
            dma((11,)),
            dma((STEPS, pairs)),
            dma((STEPS, pairs)),
            dma((2 * doms,)),
            dma((2 * doms,)),
            dma((2,)),
            dma((2,)),
            dma((2, 2)),
            dma((2, 2)),
        ],
        compiler_params=pltpu.CompilerParams(
            collective_id=0, has_side_effects=True, vmem_limit_bytes=60 * 1024 * 1024
        ),
    )(
        orbitals.reshape(2, rows, norb),
        initial.reshape(2, rows, norb),
        potential[0],
        external[0],
        occupation.reshape(1, norb),
        coupling,
        neighbours.T,
        offsets.T,
    )
    return (
        evolved.reshape(orbitals.shape),
        inter[None],
        new_grid[None],
    )


def solution(mesh):
    return jax.shard_map(
        shards,
        mesh=mesh,
        in_specs=(
            P("dom", None, "space", None, None, None),
            P("dom", None, "space", None, None, None),
            P("dom", "space", None),
            P("dom", "space", None),
            P(),
            P(),
            P(),
            P(),
        ),
        out_specs=(
            P("dom", None, "space", None, None, None),
            P("dom", None, None, None),
            P("dom", "space", None),
        ),
        check_vma=False,
    )
```

```python
import functools

import jax
import jax.numpy as jnp
from jax import lax
from jax.experimental import pallas as pl
from jax.experimental.pallas import tpu as pltpu
from jax.sharding import PartitionSpec as P

TAYLOR = 4
STEPS = 2
BUF = 4

time_step = 0.4
half_step = 0.2
xc_factor = 0.9847450218426965

F32 = jnp.float32
BF16 = jnp.bfloat16
HALO = TAYLOR


def body(
    sizes,
    orb_in,
    ini_in,
    pot_in,
    ext_in,
    occ_in,
    coup_in,
    neigh,
    offs,
    evolved_out,
    inter_out,
    pot_out,
    orb,
    ini,
    ext,
    occ,
    coup,
    packed,
    other_raw,
    halo_raw,
    other_ini,
    grids,
    source,
    term_a,
    term_b,
    term_c,
    cos_x,
    sin_x,
    field,
    odd,
    rounded,
    turned,
    sums,
    inter,
    dens,
    returned,
    load_sem,
    send_sem,
    recv_sem,
    sum_send,
    sum_recv,
    dens_send,
    dens_recv,
    swap_send,
    swap_recv,
    edge_send_sem,
    edge_recv_sem,
    step_send,
    step_recv,
    own_turned,
    other_turned,
):
    doms, space, slab, rows_y, cols_z, norb = sizes
    cells = rows_y * cols_z
    pairs = space // 2
    half = norb // 2
    main = 2 * slab
    total = main + 2 * HALO
    rows = slab * cells
    edge = HALO * cells
    cells_total = space * rows

    dom = lax.axis_index("dom")
    place = lax.axis_index("space")
    pair = place // 2
    member = place % 2
    partner = (dom, 2 * pair + 1 - member)
    has_lower = pair > 0
    has_upper = pair < pairs - 1
    outward = pair + 2 * member - 1
    has_outward = jnp.logical_and(outward >= 0, outward < pairs)
    inward = pair + 1 - 2 * member
    has_inward = jnp.logical_and(inward >= 0, inward < pairs)

    def copy(src, dst, ss, rs, device):
        return pltpu.make_async_remote_copy(
            src_ref=src,
            dst_ref=dst,
            send_sem=ss,
            recv_sem=rs,
            device_id=device,
            device_id_type=pl.DeviceIdType.MESH,
        )

    def arrived(dst, rs):
        copy(dst, dst, send_sem.at[0], rs, partner).wait_recv()

    loads = [
        pltpu.make_async_copy(src, dst, load_sem.at[k])
        for k, (src, dst) in enumerate(
            [
                (orb_in, orb),
                (pot_in, grids.at[0]),
                (ini_in, ini),
                (coup_in, coup),
                (ext_in, ext),
                (occ_in, occ),
            ]
        )
    ]
    for item in loads:
        item.start()
    barrier = pltpu.get_barrier_semaphore()

    def greet(device):
        pl.semaphore_signal(barrier, inc=1, device_id=device, device_id_type=pl.DeviceIdType.MESH)

    greet(partner)
    for step in range(1, pairs):
        greet((dom, 2 * ((pair + step) % pairs) + member))
    for step in range(1, doms):
        greet(((dom + step) % doms, 2 * pair))
        greet(((dom + step) % doms, 2 * pair + 1))

    lane = lax.broadcasted_iota(jnp.int32, (cells, norb), 1)
    left = lane < half
    sign = jnp.where(left, -1.0, 1.0).astype(F32)

    def swap(value):
        return pltpu.roll(value, half, 1)

    def at(index, count=1):
        return pl.ds(pl.multiple_of(index * cells, cells), count * cells)

    def pack_plane(j, carry):
        re = orb[0, at(j), :].astype(F32)
        im = orb[1, at(j), :].astype(F32)
        packed[0, at(j), :] = jnp.where(left, re, swap(im)).astype(BF16)
        packed[1, at(j), :] = jnp.where(left, swap(re), im).astype(BF16)
        return carry

    loads[0].wait()
    lax.fori_loop(0, slab, pack_plane, 0)
    loads[1].wait()

    pl.semaphore_wait(barrier, pairs + 2 * (doms - 1))

    grid_swap = copy(grids.at[0], grids.at[1], send_sem.at[0], recv_sem.at[0], partner)
    grid_swap.start()
    role = 1 - member
    onward = (dom, 2 * outward + member)
    back_in = (dom, 2 * inward + member)
    grid_edge = copy(
        grids.at[0], grids.at[2 + role], send_sem.at[1], recv_sem.at[1 + role], onward
    )
    grid_forward = copy(
        grids.at[1], grids.at[2 + member], send_sem.at[2], recv_sem.at[1 + member], back_in
    )

    def ranked(owner, i):
        return i + owner * (slab - 1 - 2 * i)

    def in_halo(owner, i):
        return i + owner * (HALO - 1 - 2 * i)

    raw_swap = [
        copy(
            packed.at[1 - member, at(ranked(member, i))],
            other_raw.at[at(ranked(member, i))],
            swap_send.at[i],
            swap_recv.at[i],
            partner,
        )
        for i in range(slab)
    ]
    raw_edge = [
        copy(
            packed.at[member, at(ranked(member, i))],
            halo_raw.at[role, at(in_halo(member, i))],
            edge_send_sem.at[0, i],
            edge_recv_sem.at[role, i],
            onward,
        )
        for i in range(HALO)
    ]
    raw_forward = [
        copy(
            other_raw.at[at(ranked(1 - member, i))],
            halo_raw.at[member, at(in_halo(1 - member, i))],
            edge_send_sem.at[1, i],
            edge_recv_sem.at[member, i],
            back_in,
        )
        for i in range(HALO)
    ]
    ini_swap = copy(ini, other_ini, send_sem.at[6], recv_sem.at[6], partner)
    for item in raw_swap:
        item.start()

    @pl.when(has_outward)
    def _():
        grid_edge.start()
        for item in raw_edge:
            item.start()

    zero_edge = jnp.zeros((edge, norb), BF16)

    @pl.when(jnp.logical_not(has_lower))
    def _():
        grids[2] = jnp.zeros((slab, cells), F32)
        halo_raw[0] = zero_edge
        source[1, 0:edge, :] = zero_edge

    @pl.when(jnp.logical_not(has_upper))
    def _():
        grids[3] = jnp.zeros((slab, cells), F32)
        halo_raw[1] = zero_edge
        source[1, edge + main * cells :, :] = zero_edge

    def trig_table(angle):
        count = angle.shape[0]
        fill = jnp.zeros((norb - 2 * count, cells), F32)
        return jnp.concatenate([jnp.cos(angle), jnp.sin(angle), fill], axis=0).T

    def spread(angle, planes):
        count = angle.shape[0]
        table = trig_table(angle)
        for j, plane in enumerate(planes):
            here = slice(plane * cells, (plane + 1) * cells)
            cos_x[here, :] = jnp.broadcast_to(table[:, j : j + 1], (cells, norb))
            column = table[:, count + j : count + j + 1]
            sin_x[here, :] = jnp.broadcast_to(column, (cells, norb)) * sign

    arrived(grids.at[1], recv_sem.at[0])

    @pl.when(has_inward)
    def _():
        grid_forward.start()

    is_even = member == 0
    mine, theirs = grids[0], grids[1]
    both_grids = [jnp.where(is_even, mine, theirs), jnp.where(is_even, theirs, mine)]
    spread(half_step * jnp.concatenate(both_grids, axis=0), range(HALO, HALO + main))

    def phase(value, j):
        return cos_x[at(j), :] * value - sin_x[at(j), :] * swap(value)

    def begin(value, plane):
        value = phase(value.astype(F32), plane)
        field[at(plane), :] = value
        source[0, at(plane), :] = value.astype(BF16)

    def begin_own(j, carry):
        begin(packed[member, at(j), :], HALO + member * slab + j)
        return carry

    lax.fori_loop(0, slab, begin_own, 0)
    loads[2].wait()
    for half_index in range(2):
        own_turned[half_index] = ini[half_index].T
    for i in range(slab):
        plane = ranked(1 - member, i)
        arrived(other_raw.at[at(plane)], swap_recv.at[i])
        if i < HALO:

            @pl.when(has_inward)
            def _():
                raw_forward[i].start()

        if i == slab // 2:
            ini_swap.start()

        begin(other_raw[at(plane), :], HALO + (1 - member) * slab + plane)

    z_index = lax.broadcasted_iota(jnp.int32, (rows_y, cols_z, norb), 1)
    z_first = z_index == 0
    z_last = z_index == cols_z - 1
    zero_row = jnp.zeros((1, cols_z, norb), F32)
    lower_keep = has_lower.astype(F32)
    upper_keep = has_upper.astype(F32)

    def curvature(load, j):
        center = load(j).astype(F32).reshape(rows_y, cols_z, norb)
        outer = (load(j - 1).astype(F32) + load(j + 1).astype(F32)).reshape(center.shape)
        value = outer - 6.0 * center
        value = value + jnp.concatenate([center[1:], zero_row], axis=0)
        value = value + jnp.concatenate([zero_row, center[:-1]], axis=0)
        value = value + jnp.where(z_first, 0.0, pltpu.roll(center, 1, 1))
        value = value + jnp.where(z_last, 0.0, pltpu.roll(center, cols_z - 1, 1))
        return value.reshape(cells, norb)

    loads_of = [None, term_a, term_b, term_c]

    def update_of(section, order, j, keep=None):
        factor = time_step / (2.0 * order)
        if keep is not None:
            factor = factor * keep

        def load(plane):
            if order == 1:
                return source[section, at(plane), :]
            return loads_of[order - 1][at(plane), :]

        return factor * curvature(load, j)

    def add_term(order, j, update):
        here = at(j)
        loads_of[order][here, :] = update.astype(BF16)
        if order == 1:
            odd[here, :] = update
        elif order == 2:
            field[here, :] = field[here, :] - update
        else:
            odd[here, :] = odd[here, :] - update

    def add_last(j, update):
        here = at(j)
        value = field[here, :] + update + sign * swap(odd[here, :])
        value = phase(value, j)
        field[here, :] = value
        near = value.astype(BF16)
        rounded[at(j - HALO), :] = near
        turned[at(j - HALO), :] = (-sign * swap(near.astype(F32))).astype(BF16)

    def inner_terms(section):
        for order in range(1, TAYLOR + 1):

            def pair_of_planes(i, carry, order=order):
                j, k = HALO + order + i, HALO + slab + i
                first_update = update_of(section, order, j)
                second_update = update_of(section, order, k)
                add = add_term if order < TAYLOR else lambda _, *rest: add_last(*rest)
                add(order, j, first_update)
                add(order, k, second_update)
                return carry

            if slab > order:
                lax.fori_loop(0, slab - order, pair_of_planes, 0)

    def outer_terms(section):
        def diagonal(i, carry):
            low, high = HALO - 1 - i, HALO + main + i
            if section == 0:

                @pl.when(has_lower)
                def _():
                    arrived(halo_raw.at[0, at(low)], edge_recv_sem.at[0, i])

                @pl.when(has_upper)
                def _():
                    arrived(halo_raw.at[1, at(i)], edge_recv_sem.at[1, i])

                begin(halo_raw[0, at(low), :], low)
                begin(halo_raw[1, at(i), :], high)
            else:

                @pl.when(has_lower)
                def _():
                    arrived(source.at[section, at(low)], step_recv.at[0, i])

                @pl.when(has_upper)
                def _():
                    arrived(source.at[section, at(high)], step_recv.at[1, i])

            for order in range(1, TAYLOR + 1):
                j, k = low + order, high - order
                low_keep = jnp.where(j < HALO, lower_keep, 1.0)
                high_keep = jnp.where(k >= HALO + main, upper_keep, 1.0)
                first_update = update_of(section, order, j, low_keep)
                second_update = update_of(section, order, k, high_keep)
                add = add_term if order < TAYLOR else lambda _, *rest: add_last(*rest)
                add(order, j, first_update)
                add(order, k, second_update)
            return carry

        lax.fori_loop(0, HALO, diagonal, 0)

    own_rows = pl.ds(pl.multiple_of(member * rows, cells), rows)
    other_rows = pl.ds(pl.multiple_of((1 - member) * rows, cells), rows)

    def contract(a, b):
        return jnp.dot(a, b, preferred_element_type=F32)

    def dot(a, b):
        return jnp.dot(a, b, preferred_element_type=F32)

    def correction(section, initials, owner, mixes):
        chunk = 2 if slab % 2 == 0 else 1

        def planes(j, carry):
            from_rows = pl.ds(pl.multiple_of(j * chunk * cells, cells), chunk * cells)
            place_now = owner * slab + j * chunk
            both = jnp.concatenate([initials[0, from_rows, :], initials[1, from_rows, :]], axis=1)
            gain = time_step * dot(both, mixes)
            for k in range(chunk):
                plane = HALO + place_now + k
                value = field[at(plane), :] + gain[k * cells : (k + 1) * cells]
                if section < STEPS - 1:
                    value = phase(value, plane)
                    source[section + 1, at(plane), :] = value.astype(BF16)
                else:
                    rounded[at(plane - HALO), :] = value.astype(BF16)
                field[at(plane), :] = value
            return carry

        lax.fori_loop(0, slab // chunk, planes, 0)

    def step_sends(owner, to, k):
        return [
            copy(
                source.at[1, at(HALO + owner * slab + ranked(owner, i))],
                source.at[1, at((1 - owner) * (HALO + main) + in_halo(owner, i))],
                step_send.at[k, i],
                step_recv.at[1 - owner, i],
                (dom, 2 * to + member),
            )
            for i in range(HALO)
        ]

    edge_out = step_sends(member, outward, 0)
    edge_in = step_sends(1 - member, inward, 1)
    sum_sends = []
    result = None
    for section in range(STEPS):
        inner_terms(section)
        if section == 0:

            @pl.when(has_lower)
            def _():
                arrived(grids.at[2], recv_sem.at[1])

            @pl.when(has_upper)
            def _():
                arrived(grids.at[3], recv_sem.at[2])

            ends = jnp.concatenate([grids[2, slab - HALO : slab], grids[3, 0:HALO]], axis=0)
            spread(half_step * ends, [*range(HALO), *range(HALO + main, total)])

        outer_terms(section)
        part = contract(own_turned[0], rounded[own_rows, :]) + contract(own_turned[1], turned[own_rows, :])
        if section == 0:
            arrived(other_ini, recv_sem.at[6])
            loads[3].wait()
            for half_index in range(2):
                other_turned[half_index] = other_ini[half_index].T
        part = part + contract(other_turned[0], rounded[other_rows, :])
        part = part + contract(other_turned[1], turned[other_rows, :])
        sums[section, pair] = (part * (1.0 / cells_total)).astype(sums.dtype)
        for step in range(1, pairs):
            item = copy(
                sums.at[section, pair],
                sums.at[section, pair],
                sum_send.at[section, step],
                sum_recv.at[section, pair],
                (dom, 2 * ((pair + step) % pairs) + member),
            )
            item.start()
            sum_sends.append(item)
        for step in range(1, pairs):
            slot = (pair + step) % pairs
            arrived(sums.at[section, slot], sum_recv.at[section, slot])
        result = sums[section, 0].astype(F32)
        for slot in range(1, pairs):
            result = result + sums[section, slot].astype(F32)
        mix = jnp.dot(
            coup[...], result, precision=lax.Precision.HIGHEST, preferred_element_type=F32
        )
        mix = mix.astype(BF16)
        mix_turned = (-sign[:norb] * swap(mix.astype(F32))).astype(BF16)
        mixes = jnp.concatenate([mix_turned, mix], axis=0)
        correction(section, ini, member, mixes)
        if section < STEPS - 1:

            @pl.when(has_outward)
            def _():
                for item in edge_out:
                    item.start()

        correction(section, other_ini, 1 - member, mixes)
        if section < STEPS - 1:

            @pl.when(has_inward)
            def _():
                for item in edge_in:
                    item.start()

    loads[4].wait()
    loads[5].wait()
    weight = jnp.broadcast_to(occ[...], (8, norb))
    left_8 = lax.broadcasted_iota(jnp.int32, (8, norb), 1) < half
    keep_own = jnp.logical_xor(left_8, member == 1)
    weight = jnp.where(keep_own, weight, swap(weight))[0:1]
    own_slot = 2 * dom + member
    lines = []
    for j in range(main):
        value = field[(HALO + j) * cells : (HALO + j + 1) * cells, :]
        lines.append(jnp.sum((value * value * weight).T, axis=0, keepdims=True))
    dens[own_slot] = jnp.concatenate(lines, axis=0)
    dens_sends = []
    for step in range(doms):
        for k in range(2):
            if step == 0 and k == 0:
                continue
            item = copy(
                dens.at[own_slot],
                dens.at[own_slot],
                dens_send.at[2 * step + k],
                dens_recv.at[own_slot],
                ((dom + step) % doms, 2 * pair + (member + k) % 2),
            )
            item.start()
            dens_sends.append(item)
    back = copy(rounded.at[other_rows], returned, send_sem.at[10], recv_sem.at[10], partner)
    back.start()
    inter[member] = result
    inter_swap = copy(
        inter.at[member], inter.at[member], send_sem.at[9], recv_sem.at[9], partner
    )
    inter_swap.start()
    for step in range(doms):
        for k in range(2):
            if step == 0 and k == 0:
                continue
            slot = 2 * ((dom + step) % doms) + (member + k) % 2
            arrived(dens.at[slot], dens_recv.at[slot])

    own_density = jnp.zeros((main, cells), F32)
    lower_density = jnp.zeros((main, cells), F32)
    upper_density = jnp.zeros((main, cells), F32)
    lower_owner = neigh[0, dom]
    upper_owner = neigh[1, dom]
    lower_offset = offs[0, dom]
    upper_offset = offs[1, dom]
    for d in range(doms):
        full = dens[2 * d] + dens[2 * d + 1]
        own_density = jnp.where(dom == d, full, own_density)
        lower_density = jnp.where(lower_owner == d, full, lower_density)
        upper_density = jnp.where(upper_owner == d, full, upper_density)
    low = jnp.zeros((main, cells), F32)
    high = jnp.zeros((main, cells), F32)
    for o in range(rows_y - BUF + 1):
        shift = (cells - o * cols_z) % cells
        moved = pltpu.roll(lower_density, shift, 1) if shift else lower_density
        low = jnp.where(lower_offset == o, moved, low)
        shift = (cells - BUF * cols_z - o * cols_z) % cells
        moved = pltpu.roll(upper_density, shift, 1) if shift else upper_density
        high = jnp.where(upper_offset == o, moved, high)
    y_plane = lax.broadcasted_iota(jnp.int32, (main, cells), 1) // cols_z
    from_top = y_plane - (rows_y - BUF)
    weight_low = (y_plane.astype(F32) + 1.0) / (BUF + 1.0)
    weight_high = (BUF - from_top.astype(F32)) / (BUF + 1.0)
    blended = jnp.where(
        y_plane < BUF,
        own_density * weight_low + low * (1.0 - weight_low),
        jnp.where(
            from_top >= 0, own_density * weight_high + high * (1.0 - weight_high), own_density
        ),
    )
    blended = jnp.where(is_even, blended[:slab], blended[slab:])
    root = jnp.exp(jnp.log(blended + 1e-06) * (1.0 / 3.0))
    new_grid = ext[...] - xc_factor * root
    pot_out[...] = new_grid
    table = trig_table(half_step * new_grid)
    arrived(returned, recv_sem.at[10])

    for j in range(slab):
        here = slice(j * cells, (j + 1) * cells)
        cos_v = table[:, j : j + 1]
        sin_v = table[:, slab + j : slab + j + 1]
        own_half = field[at(HALO + member * slab + j), :]
        other_half = returned[here, :].astype(F32)
        zero = jnp.where(is_even, own_half, other_half)
        one = jnp.where(is_even, other_half, own_half)
        re = jnp.where(left, zero, swap(one))
        im = jnp.where(left, swap(zero), one)
        evolved_out[0, here, :] = (cos_v * re + sin_v * im).astype(BF16)
        evolved_out[1, here, :] = (cos_v * im - sin_v * re).astype(BF16)
    arrived(inter.at[1 - member], recv_sem.at[9])
    inter_out[0] = jnp.where(left[:norb], inter[0], swap(inter[1]))
    inter_out[1] = jnp.where(left[:norb], swap(inter[0]), inter[1])

    @pl.when(has_outward)
    def _():
        for item in [grid_edge] + raw_edge:
            item.wait_send()

    @pl.when(has_outward)
    def _():
        for item in edge_out:
            item.wait_send()

    @pl.when(has_inward)
    def _():
        for item in edge_in:
            item.wait_send()
        for item in [grid_forward] + raw_forward:
            item.wait_send()

    for item in [grid_swap, ini_swap, inter_swap, back] + raw_swap + sum_sends + dens_sends:
        item.wait_send()


def shards(orbitals, initial, potential, external, occupation, coupling, neighbours, offsets):
    slab, rows_y, cols_z, norb = orbitals.shape[2:]
    doms = lax.axis_size("dom")
    space = lax.axis_size("space")
    cells = rows_y * cols_z
    rows = slab * cells
    main = 2 * slab
    total = main + 2 * HALO
    pairs = space // 2
    sizes = (doms, space, slab, rows_y, cols_z, norb)
    vmem = pl.BlockSpec(memory_space=pltpu.VMEM)
    hbm = pl.BlockSpec(memory_space=pltpu.HBM)
    smem = pl.BlockSpec(memory_space=pltpu.SMEM)
    dma = pltpu.SemaphoreType.DMA
    evolved, inter, new_grid = pl.pallas_call(
        functools.partial(body, sizes),
        out_shape=(
            jax.ShapeDtypeStruct((2, rows, norb), BF16),
            jax.ShapeDtypeStruct((2, norb, norb), F32),
            jax.ShapeDtypeStruct((slab, cells), F32),
        ),
        in_specs=[hbm] * 6 + [smem] * 2,
        out_specs=(vmem, vmem, vmem),
        scratch_shapes=[
            pltpu.VMEM((2, rows, norb), BF16),
            pltpu.VMEM((2, rows, norb), BF16),
            pltpu.VMEM((slab, cells), F32),
            pltpu.VMEM((1, norb), F32),
            pltpu.VMEM((norb, norb), F32),
            pltpu.VMEM((2, rows, norb), BF16),
            pltpu.VMEM((rows, norb), BF16),
            pltpu.VMEM((2, HALO * cells, norb), BF16),
            pltpu.VMEM((2, rows, norb), BF16),
            pltpu.VMEM((4, slab, cells), F32),
            pltpu.VMEM((STEPS, total * cells, norb), BF16),
            pltpu.VMEM((total * cells, norb), BF16),
            pltpu.VMEM((total * cells, norb), BF16),
            pltpu.VMEM((total * cells, norb), BF16),
            pltpu.VMEM((total * cells, norb), F32),
            pltpu.VMEM((total * cells, norb), F32),
            pltpu.VMEM((total * cells, norb), F32),
            pltpu.VMEM((total * cells, norb), F32),
            pltpu.VMEM((main * cells, norb), BF16),
            pltpu.VMEM((main * cells, norb), BF16),
            pltpu.VMEM((STEPS, pairs, norb, norb), BF16),
            pltpu.VMEM((2, norb, norb), F32),
            pltpu.VMEM((2 * doms, main, cells), F32),
            pltpu.VMEM((rows, norb), BF16),
            dma((6,)),
            dma((11,)),
            dma((11,)),
            dma((STEPS, pairs)),
            dma((STEPS, pairs)),
            dma((2 * doms,)),
            dma((2 * doms,)),
            dma((slab,)),
            dma((slab,)),
            dma((2, HALO)),
            dma((2, HALO)),
            dma((2, HALO)),
            dma((2, HALO)),
            pltpu.VMEM((2, norb, rows), BF16),
            pltpu.VMEM((2, norb, rows), BF16),
        ],
        compiler_params=pltpu.CompilerParams(
            collective_id=0, has_side_effects=True, vmem_limit_bytes=60 * 1024 * 1024
        ),
    )(
        orbitals.reshape(2, rows, norb),
        initial.reshape(2, rows, norb),
        potential[0],
        external[0],
        occupation.reshape(1, norb),
        coupling,
        neighbours.T,
        offsets.T,
    )
    return (
        evolved.reshape(orbitals.shape),
        inter[None],
        new_grid[None],
    )


def solution(mesh):
    return jax.shard_map(
        shards,
        mesh=mesh,
        in_specs=(
            P("dom", None, "space", None, None, None),
            P("dom", None, "space", None, None, None),
            P("dom", "space", None),
            P("dom", "space", None),
            P(),
            P(),
            P(),
            P(),
        ),
        out_specs=(
            P("dom", None, "space", None, None, None),
            P("dom", None, None, None),
            P("dom", "space", None),
        ),
        check_vma=False,
    )
```

```python
import functools

import jax
import jax.numpy as jnp
from jax import lax
from jax.experimental import pallas as pl
from jax.experimental.pallas import tpu as pltpu
from jax.sharding import PartitionSpec as P

TAYLOR = 4
STEPS = 2
BUF = 4

time_step = 0.4
half_step = 0.2
xc_factor = 0.9847450218426965

F32 = jnp.float32
BF16 = jnp.bfloat16
HALO = TAYLOR


def body(
    sizes,
    orb_in,
    ini_in,
    pot_in,
    ext_in,
    occ_in,
    coup_in,
    neigh,
    offs,
    evolved_out,
    inter_out,
    pot_out,
    orb,
    ini,
    ext,
    occ,
    coup,
    packed,
    other_raw,
    halo_raw,
    other_ini,
    grids,
    source,
    term_a,
    term_b,
    term_c,
    cos_x,
    sin_x,
    field,
    odd,
    rounded,
    turned,
    sums,
    inter,
    dens,
    returned,
    load_sem,
    send_sem,
    recv_sem,
    sum_send,
    sum_recv,
    dens_send,
    dens_recv,
    swap_send,
    swap_recv,
    edge_send_sem,
    edge_recv_sem,
    step_send,
    step_recv,
    own_turned,
    other_turned,
    evolved_store,
    inter_store,
    pot_store,
    store_sem,
):
    doms, space, slab, rows_y, cols_z, norb = sizes
    cells = rows_y * cols_z
    pairs = space // 2
    half = norb // 2
    main = 2 * slab
    total = main + 2 * HALO
    rows = slab * cells
    edge = HALO * cells
    cells_total = space * rows

    dom = lax.axis_index("dom")
    place = lax.axis_index("space")
    pair = place // 2
    member = place % 2
    partner = (dom, 2 * pair + 1 - member)
    has_lower = pair > 0
    has_upper = pair < pairs - 1
    outward = pair + 2 * member - 1
    has_outward = jnp.logical_and(outward >= 0, outward < pairs)
    inward = pair + 1 - 2 * member
    has_inward = jnp.logical_and(inward >= 0, inward < pairs)

    def copy(src, dst, ss, rs, device):
        return pltpu.make_async_remote_copy(
            src_ref=src,
            dst_ref=dst,
            send_sem=ss,
            recv_sem=rs,
            device_id=device,
            device_id_type=pl.DeviceIdType.MESH,
        )

    def arrived(dst, rs):
        copy(dst, dst, send_sem.at[0], rs, partner).wait_recv()

    loads = [
        pltpu.make_async_copy(src, dst, load_sem.at[k])
        for k, (src, dst) in enumerate(
            [
                (orb_in, orb),
                (pot_in, grids.at[0]),
                (ini_in, ini),
                (coup_in, coup),
                (ext_in, ext),
                (occ_in, occ),
            ]
        )
    ]
    for item in loads:
        item.start()
    barrier = pltpu.get_barrier_semaphore()

    def greet(device):
        pl.semaphore_signal(barrier, inc=1, device_id=device, device_id_type=pl.DeviceIdType.MESH)

    greet(partner)
    for step in range(1, pairs):
        greet((dom, 2 * ((pair + step) % pairs) + member))
    for step in range(1, doms):
        greet(((dom + step) % doms, 2 * pair))
        greet(((dom + step) % doms, 2 * pair + 1))

    lane = lax.broadcasted_iota(jnp.int32, (cells, norb), 1)
    left = lane < half
    sign = jnp.where(left, -1.0, 1.0).astype(F32)

    def swap(value):
        return pltpu.roll(value, half, 1)

    def at(index, count=1):
        return pl.ds(pl.multiple_of(index * cells, cells), count * cells)

    def pack_plane(j, carry):
        re = orb[0, at(j), :].astype(F32)
        im = orb[1, at(j), :].astype(F32)
        packed[0, at(j), :] = jnp.where(left, re, swap(im)).astype(BF16)
        packed[1, at(j), :] = jnp.where(left, swap(re), im).astype(BF16)
        return carry

    loads[0].wait()
    lax.fori_loop(0, slab, pack_plane, 0)
    loads[1].wait()

    pl.semaphore_wait(barrier, pairs + 2 * (doms - 1))

    grid_swap = copy(grids.at[0], grids.at[1], send_sem.at[0], recv_sem.at[0], partner)
    grid_swap.start()
    role = 1 - member
    onward = (dom, 2 * outward + member)
    back_in = (dom, 2 * inward + member)
    grid_edge = copy(
        grids.at[0], grids.at[2 + role], send_sem.at[1], recv_sem.at[1 + role], onward
    )
    grid_forward = copy(
        grids.at[1], grids.at[2 + member], send_sem.at[2], recv_sem.at[1 + member], back_in
    )

    def ranked(owner, i):
        return i + owner * (slab - 1 - 2 * i)

    def in_halo(owner, i):
        return i + owner * (HALO - 1 - 2 * i)

    raw_swap = [
        copy(
            packed.at[1 - member, at(ranked(member, i))],
            other_raw.at[at(ranked(member, i))],
            swap_send.at[i],
            swap_recv.at[i],
            partner,
        )
        for i in range(slab)
    ]
    raw_edge = [
        copy(
            packed.at[member, at(ranked(member, i))],
            halo_raw.at[role, at(in_halo(member, i))],
            edge_send_sem.at[0, i],
            edge_recv_sem.at[role, i],
            onward,
        )
        for i in range(HALO)
    ]
    raw_forward = [
        copy(
            other_raw.at[at(ranked(1 - member, i))],
            halo_raw.at[member, at(in_halo(1 - member, i))],
            edge_send_sem.at[1, i],
            edge_recv_sem.at[member, i],
            back_in,
        )
        for i in range(HALO)
    ]
    ini_swap = copy(ini, other_ini, send_sem.at[6], recv_sem.at[6], partner)
    for item in raw_swap:
        item.start()

    @pl.when(has_outward)
    def _():
        grid_edge.start()
        for item in raw_edge:
            item.start()

    zero_edge = jnp.zeros((edge, norb), BF16)

    @pl.when(jnp.logical_not(has_lower))
    def _():
        grids[2] = jnp.zeros((slab, cells), F32)
        halo_raw[0] = zero_edge
        source[1, 0:edge, :] = zero_edge

    @pl.when(jnp.logical_not(has_upper))
    def _():
        grids[3] = jnp.zeros((slab, cells), F32)
        halo_raw[1] = zero_edge
        source[1, edge + main * cells :, :] = zero_edge

    def trig_table(angle):
        count = angle.shape[0]
        fill = jnp.zeros((norb - 2 * count, cells), F32)
        return jnp.concatenate([jnp.cos(angle), jnp.sin(angle), fill], axis=0).T

    def spread(angle, planes):
        count = angle.shape[0]
        table = trig_table(angle)
        for j, plane in enumerate(planes):
            here = slice(plane * cells, (plane + 1) * cells)
            cos_x[here, :] = jnp.broadcast_to(table[:, j : j + 1], (cells, norb))
            column = table[:, count + j : count + j + 1]
            sin_x[here, :] = jnp.broadcast_to(column, (cells, norb)) * sign

    arrived(grids.at[1], recv_sem.at[0])

    @pl.when(has_inward)
    def _():
        grid_forward.start()

    is_even = member == 0
    mine, theirs = grids[0], grids[1]
    both_grids = [jnp.where(is_even, mine, theirs), jnp.where(is_even, theirs, mine)]
    spread(half_step * jnp.concatenate(both_grids, axis=0), range(HALO, HALO + main))

    def phase(value, j):
        return cos_x[at(j), :] * value - sin_x[at(j), :] * swap(value)

    def begin(value, plane):
        value = phase(value.astype(F32), plane)
        field[at(plane), :] = value
        source[0, at(plane), :] = value.astype(BF16)

    def begin_own(j, carry):
        begin(packed[member, at(j), :], HALO + member * slab + j)
        return carry

    lax.fori_loop(0, slab, begin_own, 0)
    loads[2].wait()
    for half_index in range(2):
        own_turned[half_index] = ini[half_index].T
    for i in range(slab):
        plane = ranked(1 - member, i)
        arrived(other_raw.at[at(plane)], swap_recv.at[i])
        if i < HALO:

            @pl.when(has_inward)
            def _():
                raw_forward[i].start()

        if i == 0:
            ini_swap.start()

        begin(other_raw[at(plane), :], HALO + (1 - member) * slab + plane)

    z_index = lax.broadcasted_iota(jnp.int32, (rows_y, cols_z, norb), 1)
    z_first = z_index == 0
    z_last = z_index == cols_z - 1
    zero_row = jnp.zeros((1, cols_z, norb), F32)
    lower_keep = has_lower.astype(F32)
    upper_keep = has_upper.astype(F32)

    def curvature(load, j):
        center = load(j).astype(F32).reshape(rows_y, cols_z, norb)
        outer = (load(j - 1).astype(F32) + load(j + 1).astype(F32)).reshape(center.shape)
        value = outer - 6.0 * center
        value = value + jnp.concatenate([center[1:], zero_row], axis=0)
        value = value + jnp.concatenate([zero_row, center[:-1]], axis=0)
        value = value + jnp.where(z_first, 0.0, pltpu.roll(center, 1, 1))
        value = value + jnp.where(z_last, 0.0, pltpu.roll(center, cols_z - 1, 1))
        return value.reshape(cells, norb)

    loads_of = [None, term_a, term_b, term_c]

    def update_of(section, order, j, keep=None):
        factor = time_step / (2.0 * order)
        if keep is not None:
            factor = factor * keep

        def load(plane):
            if order == 1:
                return source[section, at(plane), :]
            return loads_of[order - 1][at(plane), :]

        return factor * curvature(load, j)

    def add_term(order, j, update):
        here = at(j)
        loads_of[order][here, :] = update.astype(BF16)
        if order == 1:
            odd[here, :] = update
        elif order == 2:
            field[here, :] = field[here, :] - update
        else:
            odd[here, :] = odd[here, :] - update

    def add_last(j, update):
        here = at(j)
        value = field[here, :] + update + sign * swap(odd[here, :])
        value = phase(value, j)
        field[here, :] = value
        near = value.astype(BF16)
        rounded[at(j - HALO), :] = near
        turned[at(j - HALO), :] = (-sign * swap(near.astype(F32))).astype(BF16)

    def inner_terms(section):
        for order in range(1, TAYLOR + 1):

            def pair_of_planes(i, carry, order=order):
                j, k = HALO + order + i, HALO + slab + i
                first_update = update_of(section, order, j)
                second_update = update_of(section, order, k)
                add = add_term if order < TAYLOR else lambda _, *rest: add_last(*rest)
                add(order, j, first_update)
                add(order, k, second_update)
                return carry

            if slab > order:
                lax.fori_loop(0, slab - order, pair_of_planes, 0)

    def outer_terms(section):
        def diagonal(i, carry):
            low, high = HALO - 1 - i, HALO + main + i
            if section == 0:

                @pl.when(has_lower)
                def _():
                    arrived(halo_raw.at[0, at(low)], edge_recv_sem.at[0, i])

                @pl.when(has_upper)
                def _():
                    arrived(halo_raw.at[1, at(i)], edge_recv_sem.at[1, i])

                begin(halo_raw[0, at(low), :], low)
                begin(halo_raw[1, at(i), :], high)
            else:

                @pl.when(has_lower)
                def _():
                    arrived(source.at[section, at(low)], step_recv.at[0, i])

                @pl.when(has_upper)
                def _():
                    arrived(source.at[section, at(high)], step_recv.at[1, i])

            for order in range(1, TAYLOR + 1):
                j, k = low + order, high - order
                low_keep = jnp.where(j < HALO, lower_keep, 1.0)
                high_keep = jnp.where(k >= HALO + main, upper_keep, 1.0)
                first_update = update_of(section, order, j, low_keep)
                second_update = update_of(section, order, k, high_keep)
                add = add_term if order < TAYLOR else lambda _, *rest: add_last(*rest)
                add(order, j, first_update)
                add(order, k, second_update)
            return carry

        lax.fori_loop(0, HALO, diagonal, 0)

    own_rows = pl.ds(pl.multiple_of(member * rows, cells), rows)
    other_rows = pl.ds(pl.multiple_of((1 - member) * rows, cells), rows)

    def contract(a, b):
        return jnp.dot(a, b, preferred_element_type=F32)

    def dot(a, b):
        return jnp.dot(a, b, preferred_element_type=F32)

    def correction(section, initials, owner, mixes):
        chunk = 2 if slab % 2 == 0 else 1

        def planes(j, carry):
            from_rows = pl.ds(pl.multiple_of(j * chunk * cells, cells), chunk * cells)
            place_now = owner * slab + j * chunk
            both = jnp.concatenate([initials[0, from_rows, :], initials[1, from_rows, :]], axis=1)
            gain = time_step * dot(both, mixes)
            for k in range(chunk):
                plane = HALO + place_now + k
                value = field[at(plane), :] + gain[k * cells : (k + 1) * cells]
                if section < STEPS - 1:
                    value = phase(value, plane)
                    source[section + 1, at(plane), :] = value.astype(BF16)
                else:
                    rounded[at(plane - HALO), :] = value.astype(BF16)
                field[at(plane), :] = value
            return carry

        lax.fori_loop(0, slab // chunk, planes, 0)

    def step_sends(owner, to, k):
        return [
            copy(
                source.at[1, at(HALO + owner * slab + ranked(owner, i))],
                source.at[1, at((1 - owner) * (HALO + main) + in_halo(owner, i))],
                step_send.at[k, i],
                step_recv.at[1 - owner, i],
                (dom, 2 * to + member),
            )
            for i in range(HALO)
        ]

    def split(value, axis, order):
        head = value.astype(BF16)
        parts = [head, (value - head.astype(F32)).astype(BF16)]
        return jnp.concatenate([parts[k] for k in order], axis=axis)

    loads[3].wait()
    coup_parts = split(coup[...], 1, (0, 1, 0))
    edge_out = step_sends(member, outward, 0)
    edge_in = step_sends(1 - member, inward, 1)
    sum_sends = []
    result = None
    for section in range(STEPS):
        inner_terms(section)
        if section == 0:

            @pl.when(has_lower)
            def _():
                arrived(grids.at[2], recv_sem.at[1])

            @pl.when(has_upper)
            def _():
                arrived(grids.at[3], recv_sem.at[2])

            ends = jnp.concatenate([grids[2, slab - HALO : slab], grids[3, 0:HALO]], axis=0)
            spread(half_step * ends, [*range(HALO), *range(HALO + main, total)])

        outer_terms(section)
        part = contract(own_turned[0], rounded[own_rows, :]) + contract(own_turned[1], turned[own_rows, :])
        if section == 0:
            arrived(other_ini, recv_sem.at[6])
            for half_index in range(2):
                other_turned[half_index] = other_ini[half_index].T
        part = part + contract(other_turned[0], rounded[other_rows, :])
        part = part + contract(other_turned[1], turned[other_rows, :])
        sums[section, pair] = (part * (1.0 / cells_total)).astype(sums.dtype)
        for step in range(1, pairs):
            item = copy(
                sums.at[section, pair],
                sums.at[section, pair],
                sum_send.at[section, step],
                sum_recv.at[section, pair],
                (dom, 2 * ((pair + step) % pairs) + member),
            )
            item.start()
            sum_sends.append(item)
        for step in range(1, pairs):
            slot = (pair + step) % pairs
            arrived(sums.at[section, slot], sum_recv.at[section, slot])
        result = sums[section, 0].astype(F32)
        for slot in range(1, pairs):
            result = result + sums[section, slot].astype(F32)
        mix = dot(coup_parts, split(result, 0, (0, 0, 1)))
        mix = mix.astype(BF16)
        mix_turned = (-sign[:norb] * swap(mix.astype(F32))).astype(BF16)
        mixes = jnp.concatenate([mix_turned, mix], axis=0)
        if section == STEPS - 1:
            inter[member] = result
            inter_swap = copy(
                inter.at[member], inter.at[member], send_sem.at[9], recv_sem.at[9], partner
            )
            inter_swap.start()
        correction(section, ini, member, mixes)
        if section < STEPS - 1:

            @pl.when(has_outward)
            def _():
                for item in edge_out:
                    item.start()

        correction(section, other_ini, 1 - member, mixes)
        if section < STEPS - 1:

            @pl.when(has_inward)
            def _():
                for item in edge_in:
                    item.start()

    loads[4].wait()
    loads[5].wait()
    weight = jnp.broadcast_to(occ[...], (8, norb))
    left_8 = lax.broadcasted_iota(jnp.int32, (8, norb), 1) < half
    keep_own = jnp.logical_xor(left_8, member == 1)
    weight = jnp.where(keep_own, weight, swap(weight))[0:1]
    own_slot = 2 * dom + member
    lines = []
    for j in range(main):
        value = field[(HALO + j) * cells : (HALO + j + 1) * cells, :]
        lines.append(jnp.sum((value * value * weight).T, axis=0, keepdims=True))
    dens[own_slot] = jnp.concatenate(lines, axis=0)
    dens_sends = []
    for step in range(doms):
        for k in range(2):
            if step == 0 and k == 0:
                continue
            item = copy(
                dens.at[own_slot],
                dens.at[own_slot],
                dens_send.at[2 * step + k],
                dens_recv.at[own_slot],
                ((dom + step) % doms, 2 * pair + (member + k) % 2),
            )
            item.start()
            dens_sends.append(item)
    back = copy(rounded.at[other_rows], returned, send_sem.at[10], recv_sem.at[10], partner)
    back.start()
    arrived(inter.at[1 - member], recv_sem.at[9])
    inter_store[0] = jnp.where(left[:norb], inter[0], swap(inter[1]))
    inter_store[1] = jnp.where(left[:norb], swap(inter[0]), inter[1])
    stores = [pltpu.make_async_copy(inter_store, inter_out, store_sem.at[0])]
    stores[0].start()
    for step in range(doms):
        for k in range(2):
            if step == 0 and k == 0:
                continue
            slot = 2 * ((dom + step) % doms) + (member + k) % 2
            arrived(dens.at[slot], dens_recv.at[slot])

    own_density = jnp.zeros((main, cells), F32)
    lower_density = jnp.zeros((main, cells), F32)
    upper_density = jnp.zeros((main, cells), F32)
    lower_owner = neigh[0, dom]
    upper_owner = neigh[1, dom]
    lower_offset = offs[0, dom]
    upper_offset = offs[1, dom]
    for d in range(doms):
        full = dens[2 * d] + dens[2 * d + 1]
        own_density = jnp.where(dom == d, full, own_density)
        lower_density = jnp.where(lower_owner == d, full, lower_density)
        upper_density = jnp.where(upper_owner == d, full, upper_density)
    low = jnp.zeros((main, cells), F32)
    high = jnp.zeros((main, cells), F32)
    for o in range(rows_y - BUF + 1):
        shift = (cells - o * cols_z) % cells
        moved = pltpu.roll(lower_density, shift, 1) if shift else lower_density
        low = jnp.where(lower_offset == o, moved, low)
        shift = (cells - BUF * cols_z - o * cols_z) % cells
        moved = pltpu.roll(upper_density, shift, 1) if shift else upper_density
        high = jnp.where(upper_offset == o, moved, high)
    y_plane = lax.broadcasted_iota(jnp.int32, (main, cells), 1) // cols_z
    from_top = y_plane - (rows_y - BUF)
    weight_low = (y_plane.astype(F32) + 1.0) / (BUF + 1.0)
    weight_high = (BUF - from_top.astype(F32)) / (BUF + 1.0)
    blended = jnp.where(
        y_plane < BUF,
        own_density * weight_low + low * (1.0 - weight_low),
        jnp.where(
            from_top >= 0, own_density * weight_high + high * (1.0 - weight_high), own_density
        ),
    )
    blended = jnp.where(is_even, blended[:slab], blended[slab:])
    root = jnp.exp(jnp.log(blended + 1e-06) * (1.0 / 3.0))
    new_grid = ext[...] - xc_factor * root
    pot_store[...] = new_grid
    stores.append(pltpu.make_async_copy(pot_store, pot_out, store_sem.at[1]))
    stores[1].start()
    table = trig_table(half_step * new_grid)
    arrived(returned, recv_sem.at[10])

    for j in range(slab):
        here = slice(j * cells, (j + 1) * cells)
        cos_v = table[:, j : j + 1]
        sin_v = table[:, slab + j : slab + j + 1]
        own_half = field[at(HALO + member * slab + j), :]
        other_half = returned[here, :].astype(F32)
        zero = jnp.where(is_even, own_half, other_half)
        one = jnp.where(is_even, other_half, own_half)
        re = jnp.where(left, zero, swap(one))
        im = jnp.where(left, swap(zero), one)
        evolved_store[0, here, :] = (cos_v * re + sin_v * im).astype(BF16)
        evolved_store[1, here, :] = (cos_v * im - sin_v * re).astype(BF16)
        for part in range(2):
            item = pltpu.make_async_copy(
                evolved_store.at[part, here],
                evolved_out.at[part, here],
                store_sem.at[2 + 2 * j + part],
            )
            item.start()
            stores.append(item)
    for item in stores:
        item.wait()
    @pl.when(has_outward)
    def _():
        for item in [grid_edge] + raw_edge:
            item.wait_send()

    @pl.when(has_outward)
    def _():
        for item in edge_out:
            item.wait_send()

    @pl.when(has_inward)
    def _():
        for item in edge_in:
            item.wait_send()
        for item in [grid_forward] + raw_forward:
            item.wait_send()

    for item in [grid_swap, ini_swap, inter_swap, back] + raw_swap + sum_sends + dens_sends:
        item.wait_send()


def shards(orbitals, initial, potential, external, occupation, coupling, neighbours, offsets):
    slab, rows_y, cols_z, norb = orbitals.shape[2:]
    doms = lax.axis_size("dom")
    space = lax.axis_size("space")
    cells = rows_y * cols_z
    rows = slab * cells
    main = 2 * slab
    total = main + 2 * HALO
    pairs = space // 2
    sizes = (doms, space, slab, rows_y, cols_z, norb)
    hbm = pl.BlockSpec(memory_space=pltpu.HBM)
    smem = pl.BlockSpec(memory_space=pltpu.SMEM)
    dma = pltpu.SemaphoreType.DMA
    evolved, inter, new_grid = pl.pallas_call(
        functools.partial(body, sizes),
        out_shape=(
            jax.ShapeDtypeStruct((2, rows, norb), BF16),
            jax.ShapeDtypeStruct((2, norb, norb), F32),
            jax.ShapeDtypeStruct((slab, cells), F32),
        ),
        in_specs=[hbm] * 6 + [smem] * 2,
        out_specs=(hbm, hbm, hbm),
        scratch_shapes=[
            pltpu.VMEM((2, rows, norb), BF16),
            pltpu.VMEM((2, rows, norb), BF16),
            pltpu.VMEM((slab, cells), F32),
            pltpu.VMEM((1, norb), F32),
            pltpu.VMEM((norb, norb), F32),
            pltpu.VMEM((2, rows, norb), BF16),
            pltpu.VMEM((rows, norb), BF16),
            pltpu.VMEM((2, HALO * cells, norb), BF16),
            pltpu.VMEM((2, rows, norb), BF16),
            pltpu.VMEM((4, slab, cells), F32),
            pltpu.VMEM((STEPS, total * cells, norb), BF16),
            pltpu.VMEM((total * cells, norb), BF16),
            pltpu.VMEM((total * cells, norb), BF16),
            pltpu.VMEM((total * cells, norb), BF16),
            pltpu.VMEM((total * cells, norb), F32),
            pltpu.VMEM((total * cells, norb), F32),
            pltpu.VMEM((total * cells, norb), F32),
            pltpu.VMEM((total * cells, norb), F32),
            pltpu.VMEM((main * cells, norb), BF16),
            pltpu.VMEM((main * cells, norb), BF16),
            pltpu.VMEM((STEPS, pairs, norb, norb), BF16),
            pltpu.VMEM((2, norb, norb), F32),
            pltpu.VMEM((2 * doms, main, cells), F32),
            pltpu.VMEM((rows, norb), BF16),
            dma((6,)),
            dma((11,)),
            dma((11,)),
            dma((STEPS, pairs)),
            dma((STEPS, pairs)),
            dma((2 * doms,)),
            dma((2 * doms,)),
            dma((slab,)),
            dma((slab,)),
            dma((2, HALO)),
            dma((2, HALO)),
            dma((2, HALO)),
            dma((2, HALO)),
            pltpu.VMEM((2, norb, rows), BF16),
            pltpu.VMEM((2, norb, rows), BF16),
            pltpu.VMEM((2, rows, norb), BF16),
            pltpu.VMEM((2, norb, norb), F32),
            pltpu.VMEM((slab, cells), F32),
            dma((2 + 2 * slab,)),
        ],
        compiler_params=pltpu.CompilerParams(
            collective_id=0, has_side_effects=True, vmem_limit_bytes=60 * 1024 * 1024
        ),
    )(
        orbitals.reshape(2, rows, norb),
        initial.reshape(2, rows, norb),
        potential[0],
        external[0],
        occupation.reshape(1, norb),
        coupling,
        neighbours.T,
        offsets.T,
    )
    return (
        evolved.reshape(orbitals.shape),
        inter[None],
        new_grid[None],
    )


def solution(mesh):
    return jax.shard_map(
        shards,
        mesh=mesh,
        in_specs=(
            P("dom", None, "space", None, None, None),
            P("dom", None, "space", None, None, None),
            P("dom", "space", None),
            P("dom", "space", None),
            P(),
            P(),
            P(),
            P(),
        ),
        out_specs=(
            P("dom", None, "space", None, None, None),
            P("dom", None, None, None),
            P("dom", "space", None),
        ),
        check_vma=False,
    )
```
